32 devices in a mesh: layer: 4 (over y, core), expert: 8 (over z, x).
Axes of the slice: x: 2, y: 2, z: 4, core: 2. Of those that a mesh axis runs over, the one named last changes fastest.
Arguments:
- stream_in: bfloat16 [4, 256, 3584], P(None, 'expert'), may hold values from -6 to 6
- gain: float32 [4, 3584], P('layer'), may hold values from 0.5 to 1.5
- w_gate: bfloat16 [4, 3584, 2048], P('layer', None, 'expert'), may hold values from -0.09375 to 0.09375
- w_up: bfloat16 [4, 3584, 2048], P('layer', None, 'expert'), may hold values from -0.09375 to 0.09375
- w_down: bfloat16 [4, 2048, 3584], P('layer', 'expert'), may hold values from -0.125 to 0.125
- routes: int32 [4, 4, 256, 8], P('layer', None, 'expert'), may hold values from 0 to 255, all different within a row; in each aligned block of 32 rows (0 to 31, 32 to 63, ..., all dimensions but the last counted through in order) at most 2 rows name the same one
- gates: float32 [4, 4, 256, 8], P('layer', None, 'expert'), may hold values from 0.2 to 1
Outputs:
- layer_out: bfloat16 [4, 4, 256, 3584], P('layer', None, 'expert')
- hessian: float32 [4, 2048, 2048], P('layer', 'expert')
The draws below stay inside these ranges and needn't reach their ends.
Inputs may be any that keep to these rules, and one draw needn't show every extreme that they name: `routes`: each token names 8 different experts; in each aligned block of 32 tokens (the rows of one device) no expert is named by more than 2 tokens.
All inputs are finite; a program needn't handle non-finite values.
Results may differ from the reference program's by a relative error of at most 0.014.
Values may be sent and summed in bfloat16 or wider, within the bound.
No kernel may reach another device: no remote copies, remote signals or barrier semaphores. Data moves between devices by JAX's collectives and lax.ppermute only.
A program may use at most 64 MiB of HBM per device.

```python
import math
import jax
import jax.numpy as jnp
import numpy as np
from jax import lax

D = 3584
FF = 2048
EXPERTS = 256
TOP = 8
GROUP = 8
FRONTS = 4
TOK_DEV = 32
CAP = 2
LAYERS = 4
FLIGHT = 1
TOKENS = 256
N_EXPERT = 8


def block_scale(rng, shape, cuts, low, top_value):
    level = 1.0
    for axis_at, blocks in cuts:
        steps = jax.random.uniform(jax.random.fold_in(jax.random.fold_in(rng, 6), axis_at), (blocks,), jnp.float32, low / len(cuts), top_value / len(cuts))
        level = level * jnp.repeat(jnp.exp(steps), shape[axis_at] // blocks).reshape((-1,) + (1,) * (len(shape) - 1 - axis_at))
    return level


def routed_block(own_key, own, number, rows, count, top, reach, skew):
    sequence = jax.random.permutation(own_key, count)
    packed, ordinary = shares(count, rows * top, reach, skew, True), shares(count, rows * top, reach, skew, False)
    places = jnp.arange(count)

    def named(sizes, turn):
        used = int((sizes > 0).sum())
        fixed = max(1, used // 4)
        passed = fixed + (places - fixed + turn * (used - fixed)) % max(1, count - fixed)
        return jnp.zeros((count,), jnp.int32).at[sequence[jnp.where(places < fixed, places, passed)]].set(jnp.asarray(sizes, jnp.int32))

    sizes = jnp.where(number % 4 == 0, named(packed, number // 4), named(ordinary, number - number // 4 - 1))
    mixed = jax.random.permutation(jax.random.fold_in(own, 3), count)
    source_of, taker = mixed[0:count // 2 * 2:2], mixed[1:count // 2 * 2:2]
    room = jnp.minimum(sizes[source_of] - 1, reach - sizes[taker]) // 2
    room = jnp.where((source_of == sequence[0]) | (taker == sequence[0]) | (sizes[taker] == 0), 0, jnp.maximum(room, 0))
    passed = jax.random.randint(jax.random.fold_in(own, 4), (count // 2,), 0, 1 << 20) % (room + 1)
    sizes = sizes.at[source_of].add(-passed).at[taker].add(passed)
    items = jnp.searchsorted(jnp.cumsum(sizes), jnp.arange(rows * top), side="right").astype(jnp.int32)
    table = items.reshape(top, rows).T
    table = table[jax.random.permutation(jax.random.fold_in(own, 1), rows)]
    turn = jax.random.randint(jax.random.fold_in(own, 2), (rows, 1), 0, top)
    return jnp.take_along_axis(table, (jnp.arange(top)[None, :] + turn) % top, axis=1)


def shares(count, total, reach, slope, full):
    weights = [(1 << 20) // math.isqrt(standing ** slope) + 1 for standing in range(1, count + 1)]
    largest = reach if full else min(reach, max(-(-total // count), total * weights[0] // sum(weights)))
    least = 1 if total - largest >= count - 1 else 0
    counts, spare = [largest] + [least] * (count - 1), total - largest - least * (count - 1)
    while spare > 0:
        free = [i for i in range(1, count) if counts[i] < largest] or [i for i in range(1, count) if counts[i] < reach]
        whole, remaining = sum([weights[i] for i in free]), spare
        for i in free:
            addition = min(reach - counts[i], max(1, remaining * weights[i] // whole), spare)
            counts[i] = counts[i] + addition
            spare = spare - addition
    return np.array(counts)


def normal_values(key, dims, scale, limit, cuts=(), held_as=jnp.bfloat16):
    drawn = scale * jax.random.normal(key, dims, jnp.float32)
    if cuts:
        drawn = drawn * block_scale(key, dims, cuts, -0.22, 0.18)
    return jnp.clip(drawn, -limit, limit).astype(held_as)


def setup_inputs(seed: int = 0) -> dict:
    key_of = jax.random.split(jax.random.key(seed), 8)
    stream_in = normal_values(key_of[0], (FRONTS, TOKENS, D), 1.0, 6.0, ((1, 8),))
    gain = jnp.clip(1.0 + 0.1 * jax.random.normal(key_of[1], (LAYERS, D), jnp.float32), 0.5, 1.5)
    w_gate = normal_values(key_of[2], (LAYERS, D, FLIGHT * FF), D ** -0.5, 0.09375, ((0, 4), (2, 8)))
    w_up = normal_values(key_of[3], (LAYERS, D, FLIGHT * FF), D ** -0.5, 0.09375, ((0, 4), (2, 8)))
    w_down = normal_values(key_of[4], (LAYERS, FLIGHT * FF, D), FF ** -0.5, 0.125, ((0, 4), (1, 8)))
    routes_keys = jax.random.split(jax.random.fold_in(key_of[5], 1), LAYERS * FRONTS * TOKENS // TOK_DEV)
    routes_turns = jax.random.permutation(jax.random.fold_in(key_of[5], 3), LAYERS * FRONTS * TOKENS // TOK_DEV)
    routes = jax.vmap(lambda own, number: routed_block(jax.random.fold_in(key_of[5], 2), own, number, TOK_DEV, EXPERTS, TOP, CAP, 2))(routes_keys, routes_turns).reshape((LAYERS, FRONTS, TOKENS, TOP))
    gates = jnp.clip(0.2 + 0.8 * jax.random.uniform(key_of[6], (LAYERS, FRONTS, TOKENS, TOP), jnp.float32) ** block_scale(key_of[6], (LAYERS, FRONTS, TOKENS, TOP), ((0, 4), (2, 8)), -0.2, 0.2), 0.2, 1.0)
    return {"stream_in": stream_in, "gain": gain, "w_gate": w_gate, "w_up": w_up, "w_down": w_down, "routes": routes, "gates": gates}


EPSILON = 1e-06

def reference(stream_in, gain, w_gate, w_up, w_down, routes, gates):
    flight = N_EXPERT // GROUP
    units = FF // GROUP
    rows_all = N_EXPERT * CAP
    state = stream_in
    layer_outputs = []
    grams = []
    for layer in range(LAYERS):
        gram_parts = [jnp.zeros((FF, FF), jnp.float32) for expert in range(flight)]
        fronts_out = []
        for front in range(FRONTS):
            wide = state[front].astype(jnp.float32)
            scale = lax.rsqrt(lax.optimization_barrier(jnp.mean(wide * wide, axis=-1, keepdims=True)) + EPSILON)
            normed = (wide * scale * gain[layer]).astype(jnp.bfloat16)
            update = jnp.zeros((TOKENS, D), jnp.float32)
            for expert in range(flight):
                matches = routes[layer, front] == expert
                routed = jnp.any(matches, axis=1)
                weight = lax.optimization_barrier(jnp.sum(jnp.where(matches, gates[layer, front], 0.0), axis=1))
                blocks = routed.astype(jnp.int32).reshape(N_EXPERT, TOK_DEV)
                place = (jnp.cumsum(blocks, axis=1) - 1).reshape(TOKENS).astype(jnp.int32)
                owner = jnp.arange(TOKENS, dtype=jnp.int32) // TOK_DEV
                target = jnp.where(routed, owner * CAP + place, rows_all).astype(jnp.int32)
                gathered = jnp.zeros((rows_all + 1, D), jnp.bfloat16).at[target].set(normed)[:rows_all]
                low = expert * FF
                gate_act = jnp.dot(gathered, w_gate[layer][:, low:low + FF], preferred_element_type=jnp.float32)
                up_act = jnp.dot(gathered, w_up[layer][:, low:low + FF], preferred_element_type=jnp.float32)
                hidden = (jax.nn.silu(gate_act) * up_act).astype(jnp.bfloat16)
                gram_parts[expert] = gram_parts[expert] + jnp.dot(hidden.T, hidden, preferred_element_type=jnp.float32)
                total = jnp.zeros((rows_all, D), jnp.float32)
                for member in range(GROUP):
                    first = low + member * units
                    piece = jnp.dot(hidden[:, member * units:(member + 1) * units], w_down[layer][first:first + units], preferred_element_type=jnp.float32).astype(jnp.bfloat16)
                    total = total + lax.optimization_barrier(piece).astype(jnp.float32)
                padded = jnp.concatenate([total, jnp.zeros((1, D), jnp.float32)], axis=0)
                update = update + weight[:, None] * padded[target]
            fronts_out.append((wide + update).astype(jnp.bfloat16))
        state = jnp.stack(fronts_out)
        layer_outputs.append(state)
        grams.append(jnp.concatenate(gram_parts, axis=0) * (1.0 / (FRONTS * CAP)))
    return (jnp.stack(layer_outputs), jnp.stack(grams))
```

```python
import functools

import jax
import jax.numpy as jnp
from jax import lax
from jax.experimental import pallas as pl
from jax.experimental.pallas import tpu as pltpu
from jax.sharding import PartitionSpec as P

GROUP = 8
CAP = 2
EPSILON = 1e-06
LANES = 128
CHUNK = 128

FEW = 4

STATUS, SOURCE_LAYER, SOURCE_SLOT, WANTED, FULL, DEEP, DEVICE, SLOT, MORE, COUNTS = range(64, 74)
READY, WAITS = 1.0, 2.0

f32 = jnp.float32
bf16 = jnp.bfloat16
VMEM = pl.BlockSpec(memory_space=pltpu.VMEM)
SMEM = pl.BlockSpec(memory_space=pltpu.SMEM)
HBM = pl.BlockSpec(memory_space=pltpu.HBM)


def call(
    body, out_shape, n_in, scalars=0, scratch=(), flops=0, traffic=0, limit=2 * 2**20, streamed=0, placed=None
):
    return pl.pallas_call(
        body,
        out_shape=out_shape,
        in_specs=[SMEM] * scalars + [VMEM] * n_in + [HBM] * streamed,
        out_specs=placed or jax.tree.map(lambda s: VMEM, out_shape),
        scratch_shapes=list(scratch),
        compiler_params=pltpu.CompilerParams(vmem_limit_bytes=limit),
        cost_estimate=pl.CostEstimate(flops=flops, bytes_accessed=traffic, transcendentals=0),
    )


def iota(shape, dim):
    return lax.broadcasted_iota(jnp.int32, shape, dim)


def stack_rows(rows):
    return jnp.concatenate(rows, axis=0)


def lane_of(extra, number):
    return extra[:, number:number + 1]


def across(column):
    size = column.shape[0]
    same = iota((size, size), 0) == iota((size, size), 1)
    return jnp.sum(jnp.where(same, column, 0.0), axis=0, keepdims=True)


def ranked(rows):
    size = rows[0].shape[1]
    upto = (iota((size, size), 0) <= iota((size, size), 1)).astype(f32).astype(bf16)
    rank = jnp.dot(stack_rows(rows).astype(bf16), upto, preferred_element_type=f32)
    return [rank[r:r + 1] * row for r, row in enumerate(rows)]


def selection(rank, count):
    wanted = (iota((count, rank.shape[1]), 0) + 1).astype(f32)
    return jnp.where(rank == wanted, 1.0, 0.0)


def normalized(rows, gain):
    scale = lax.rsqrt(jnp.mean(rows * rows, axis=-1, keepdims=True) + EPSILON)
    return (rows * scale * gain).astype(bf16)


def by_front(routes_ref, of_front):
    return jnp.concatenate([of_front(f) for f in range(routes_ref.shape[0])], axis=1)


def table_body(flight, routes_ref, table_ref, kept_ref):
    kept_ref[...] = routes_ref[...]
    table_ref[...] = by_front(
        routes_ref,
        lambda f: jnp.max(jnp.where(routes_ref[f] < flight, 1.0, 0.0), axis=0, keepdims=True),
    ).astype(bf16)


def held_body(after_ref, *refs):
    count = len(refs) // 2
    sems = refs[-1]
    copies = [pltpu.make_async_copy(refs[i], refs[count + i], sems.at[i]) for i in range(count)]
    for copy in copies:
        copy.start()
    for copy in copies:
        copy.wait()


def rows_body(table_ref, state_ref, raw_ref):
    select = selection(ranked([table_ref[...].astype(f32)])[0], raw_ref.shape[0])
    raw_ref[...] = jnp.dot(select.astype(bf16), state_ref[...], preferred_element_type=f32).astype(bf16)


def gates_body(routes_ref, gates_ref, weights_ref):
    weights_ref[...] = stack_rows([
        by_front(
            routes_ref,
            lambda f: jnp.sum(jnp.where(routes_ref[f] == expert, gates_ref[f], 0.0), axis=0, keepdims=True),
        )
        for expert in range(weights_ref.shape[0])
    ])


def before(layer, a, b):
    return jnp.where((layer ^ a) < (layer ^ b), 1.0, 0.0)


def between(layer, a, b, routed):
    total = jnp.zeros_like(routed[0])
    for r, row in enumerate(routed):
        if r not in (a, b):
            total = jnp.maximum(total, row * before(layer, a, r) * before(layer, r, b))
    return total


def number_of(layer, r, sections):
    return sum(jnp.where((layer ^ r) == other, float(other), 0.0) for other in range(sections))


def meta_body(few, index_ref, *refs):
    tables, (gates_ref, raw_ref, payload_ref) = refs[:-3], refs[-3:]
    layer, member = index_ref[0], index_ref[1]
    count, width = raw_ref.shape
    routed = [ref[...].astype(f32) for ref in tables]
    ranks = ranked(routed)
    waits = source_layer = source_slot = wanted = jnp.zeros_like(routed[0])
    for r in range(1, len(routed)):
        source = routed[r] * before(layer, r, 0) * (1.0 - between(layer, r, 0, routed))
        waits = waits + source
        source_layer = source_layer + source * number_of(layer, r, len(routed))
        source_slot = source_slot + source * ranks[r]
        wanted = jnp.maximum(wanted, routed[r] * before(layer, 0, r))
    status = jnp.where(waits > 0.5, WAITS, READY)
    full = sum(jnp.where(rank > few, 1.0, 0.0) for rank in ranks)
    deep = jnp.where(sum(routed) > 2.5, 1.0, 0.0)
    counts = [jnp.zeros_like(deep) for _ in routed]
    for r, row in enumerate(routed):
        later = jnp.zeros_like(row)
        for other, other_row in enumerate(routed):
            if other != r:
                later = jnp.maximum(later, other_row * before(layer, r, other))
        for place in range(len(counts)):
            counts[place] = counts[place] + row * later * jnp.where((layer ^ r) == place, 1.0, 0.0)
    gates = gates_ref[...]
    high = gates.astype(bf16).astype(f32)
    named = {STATUS: status, SOURCE_LAYER: source_layer, SOURCE_SLOT: source_slot, WANTED: wanted}
    summed = {FULL: full, DEEP: deep}
    summed.update({COUNTS + place: row for place, row in enumerate(counts)})
    for expert in range(gates.shape[0]):
        named[expert] = high[expert:expert + 1]
        named[gates.shape[0] + expert] = (gates - high)[expert:expert + 1]
    select = selection(ranks[0], count)
    across_tokens = (((1,), (1,)), ((), ()))

    def lanes(left, rows):
        empty = jnp.zeros_like(deep)
        table = stack_rows([rows.get(lane, empty) for lane in range(LANES)]).astype(bf16)
        return lax.dot_general(left.astype(bf16), table, across_tokens, preferred_element_type=f32)

    lane = iota((count, LANES), 1)
    extra = lanes(select, named) + lanes(jnp.ones_like(select), summed)
    extra = jnp.where(lane == DEVICE, jnp.full((count, LANES), member + 1, jnp.int32).astype(f32), extra)
    extra = jnp.where(lane == SLOT, (iota((count, LANES), 0) + 1).astype(f32), extra)
    payload_ref[:, :width] = raw_ref[...]
    payload_ref[:, width:] = extra.astype(bf16)


def distances(half):
    return [2 * q for q in range(half)] + [2 * q + 1 for q in range(half)]


def stack_body(half, *refs):
    near, pair_ref, rows_ref = refs[:half], refs[half], refs[half + 1]
    blocks = [ref[...] for ref in near] + [pair_ref[q] for q in range(half)]
    count = blocks[0].shape[0]
    if count % 16 == 0:
        for place, block in enumerate(blocks):
            rows_ref[place * count:(place + 1) * count] = block
    else:
        rows_ref[...] = stack_rows([block.astype(f32) for block in blocks]).astype(bf16)


def first_pass_body(half, sections, count, flight, member_ref, *refs):
    gathered, refs = refs[:half + 1], refs[half + 1:]
    gain_ref, gate_ref, up_ref, down_ref, rows_ref, mode_ref, part_ref, chosen_ref, sent_ref = refs
    stack_body(half, *gathered, rows_ref)
    pass_body(count, flight, member_ref, rows_ref, gain_ref, gate_ref, up_ref, down_ref, part_ref, chosen_ref, sent_ref)
    extra = rows_ref[:, gain_ref.shape[1]:].astype(f32)
    most = jnp.max(extra, axis=0, keepdims=True)
    total = jnp.sum(jnp.where(lane_of(extra, SLOT) == 1.0, extra, 0.0), axis=0, keepdims=True)
    total = jnp.max(total[:, COUNTS:COUNTS + sections], axis=1, keepdims=True)
    wanted_count = part_ref.shape[0]
    mode = sum(jnp.where(total > limit, 1, 0) for limit in (wanted_count // 4, wanted_count // 2, wanted_count))
    mode = jnp.where(lane_of(most, DEEP) > 0.5, 3, mode)
    mode_ref[...] = jnp.where(lane_of(most, FULL) > 0.5, 4, mode)


def activated(rows, gate_ref, up_ref):
    gate = jnp.dot(rows, gate_ref[...], preferred_element_type=f32)
    up = jnp.dot(rows, up_ref[...], preferred_element_type=f32)
    return gate / (1.0 + jnp.exp(-gate)) * up


def weight_of(extra, member, flight):
    lane = iota(extra.shape, 1)
    expert = member // GROUP
    mine = jnp.logical_or(lane == expert, lane == flight + expert)
    return jnp.sum(jnp.where(mine, extra, 0.0), axis=1, keepdims=True)


def pass_body(count, flight, member_ref, rows_ref, gain_ref, gate_ref, up_ref, down_ref, part_ref, chosen_ref, sent_ref):
    member = member_ref[0]
    width = gain_ref.shape[1]
    wanted_count = part_ref.shape[0]
    extra = rows_ref[:, width:].astype(f32)
    wanted = lane_of(extra, WANTED)
    eligible = jnp.where(lane_of(extra, STATUS) == READY, wanted, 0.0)
    number = lane_of(extra, DEVICE) * count + lane_of(extra, SLOT)
    upto = number <= across(number)
    rank = jnp.sum(jnp.where(upto, eligible, 0.0), axis=0, keepdims=True) * across(eligible)
    select = selection(rank, wanted_count)
    chosen = jnp.dot(select.astype(bf16), rows_ref[...], preferred_element_type=f32)
    taken = jnp.sum(select, axis=0, keepdims=True)
    more = jnp.max(across(wanted) - taken, axis=1, keepdims=True)
    sent_ref[...] = taken
    lanes = chosen[:, width:]
    lane = iota(lanes.shape, 1)
    chosen_ref[:, :width] = chosen[:, :width].astype(bf16)
    chosen_ref[:, width:] = jnp.where(lane == MORE, more, lanes).astype(bf16)
    weight = weight_of(lanes, member, flight)
    hidden = activated(normalized(chosen[:, :width], gain_ref[...]), gate_ref, up_ref)
    if flight > 1:
        hidden = jnp.where(weight > 0.0, hidden, 0.0)
    share = jnp.dot(hidden.astype(bf16), down_ref[...], preferred_element_type=f32) * weight
    part_ref[...] = share.astype(bf16)


def added_body(a_ref, b_ref, out_ref):
    out_ref[...] = (a_ref[...].astype(f32) + b_ref[...].astype(f32)).astype(bf16)


def changed_body(a_ref, b_ref, chosen_ref, out_ref):
    width = a_ref.shape[1]
    total = chosen_ref[:, :width].astype(f32) + a_ref[...].astype(f32) + b_ref[...].astype(f32)
    out_ref[:, :width] = total.astype(bf16)
    out_ref[:, width:] = chosen_ref[:, width:]


def by_chunks(size, run):
    if size <= CHUNK:
        run(slice(0, size))
        return

    @pl.loop(0, size // CHUNK)
    def _(i):
        run(pl.ds(pl.multiple_of(i * CHUNK, CHUNK), CHUNK))


def apply_body(sections, layer_ref, rows_ref, sent_ref, *refs):
    changed, into_ref, more_ref = refs[:sections], refs[sections], refs[sections + 1]
    layer = layer_ref[0]
    width = rows_ref.shape[1] - LANES
    names = [ref[:, width:].astype(f32) for ref in changed]
    fresh = stack_rows([ref[:, :width].astype(f32) for ref in changed[1:]]).astype(bf16)
    columns = [(across(lane_of(name, DEVICE)), across(lane_of(name, SLOT))) for name in names]
    more = names[0]
    for name in names[1:]:
        more = jnp.maximum(more, name)
    more_ref[...] = jnp.max(lane_of(more, MORE), axis=0, keepdims=True)
    size = rows_ref.shape[0]
    taken = sent_ref[...]

    def run(part):
        extra = rows_ref[part, width:].astype(f32)
        waits = jnp.where(lane_of(extra, STATUS) == WAITS, 1.0, 0.0)
        matches = []
        for r in range(1, sections):
            device, slot = columns[r]
            match = jnp.where(lane_of(extra, DEVICE) == device, waits, 0.0)
            match = match * jnp.where(lane_of(extra, SOURCE_SLOT) == slot, 1.0, 0.0)
            from_it = jnp.where(lane_of(extra, SOURCE_LAYER) == number_of(layer, r, sections), 1.0, 0.0)
            matches.append(match * from_it)
        match = jnp.concatenate(matches, axis=1)
        arrived = jnp.max(match, axis=1, keepdims=True)
        new = jnp.dot(match.astype(bf16), fresh, preferred_element_type=f32)
        old = rows_ref[part, :width].astype(f32)
        into_ref[part, :width] = jnp.where(arrived > 0.5, new, old).astype(bf16)
        lane = iota(extra.shape, 1)
        extra = jnp.where(jnp.logical_and(lane == STATUS, arrived > 0.5), READY, extra)
        if size <= CHUNK:
            own = iota((size, size), 0) == iota((size, size), 1)
            gone = jnp.sum(jnp.where(own, taken, 0.0), axis=1, keepdims=True)
        else:
            first = part.start
            row = iota((CHUNK, size), 0) + first == iota((CHUNK, size), 1)
            gone = jnp.sum(jnp.where(row, taken, 0.0), axis=1, keepdims=True)
        extra = jnp.where(jnp.logical_and(lane == WANTED, gone > 0.5), 0.0, extra)
        into_ref[part, width:] = extra.astype(bf16)

    by_chunks(size, run)


def changed_final_body(half, sections, flight, layer_ref, member_ref, rows_ref, sent_ref, *refs):
    changed, rest, scratch = refs[:sections], refs[sections:-2], refs[-2:]
    into_ref, more_ref = scratch
    apply_body(sections, layer_ref, rows_ref, sent_ref, *changed, into_ref, more_ref)
    final_body(half, flight, member_ref, into_ref, *rest)


def final_body(half, flight, member_ref, rows_ref, gain_ref, gate_ref, up_ref, down_ref, hidden_ref, raw_ref, near_ref, far_ref, ordered_ref):
    member = member_ref[0]
    width = gain_ref.shape[1]
    units = hidden_ref.shape[1]
    size = rows_ref.shape[0]
    side = size // 2
    count = raw_ref.shape[0]
    raw_ref[...] = rows_ref[:, :width].astype(f32)[:count].astype(bf16) if size <= CHUNK else rows_ref[:count, :width]
    hidden_rows = []

    def run(part, of_part=None):
        extra = rows_ref[part, width:].astype(f32)
        weight = weight_of(extra, member, flight)
        hidden = activated(normalized(rows_ref[part, :width].astype(f32), gain_ref[...]), gate_ref, up_ref)
        if flight > 1:
            hidden = jnp.where(weight > 0.0, hidden, 0.0)
        share = jnp.dot(hidden.astype(bf16), down_ref[...], preferred_element_type=f32) * weight
        return hidden, share.astype(bf16)

    if size <= CHUNK:
        hidden, share = run(slice(0, size))
        near_ref[...] = share[:side]
        far_ref[:, :width] = share[side:]
        for place, r in enumerate(distances(half)):
            ordered_ref[member ^ r, :count] = hidden[place * count:(place + 1) * count]
    else:
        blocks = CHUNK // count

        def half_run(first, into_ref, odd):
            @pl.loop(0, side // CHUNK)
            def _(i):
                at = pl.multiple_of(i * CHUNK, CHUNK)
                hidden, share = run(pl.ds(pl.multiple_of(first + at, CHUNK), CHUNK))
                into_ref[pl.ds(at, CHUNK), :width] = share
                for b in range(blocks):
                    ordered_ref[member ^ (2 * (i * blocks + b) + odd)] = hidden[b * count:(b + 1) * count]

        half_run(0, near_ref, 0)
        half_run(side, far_ref, 1)
    hidden_rows = stack_rows([ordered_ref[source, :count] for source in range(2 * half)]).astype(bf16)
    hidden_ref[...] = hidden_rows
    far_ref[:, width:width + units] = hidden_rows[:side]
    far_ref[:, width + units:] = hidden_rows[side:]


def regrouped(rows, count):
    return jnp.concatenate([rows[i:i + count] for i in range(0, rows.shape[0], count)], axis=1)


def spread(block, units):
    return stack_rows([block[:, i:i + units] for i in range(0, block.shape[1], units)])


def paired_body(half, near_ref, far_ref, hidden_ref, *out_refs):
    width = near_ref.shape[1]
    units = hidden_ref.shape[1]
    count = near_ref.shape[0] // half
    total = near_ref[...].astype(f32) + far_ref[:, :width].astype(f32)
    theirs = far_ref[:, width:].astype(f32)
    both = [hidden_ref[...].astype(f32), theirs[:, :units], theirs[:, units:]]
    both = jnp.concatenate([regrouped(rows, count) for rows in both], axis=1).astype(bf16)
    for q, ref in enumerate(out_refs):
        ref[:, :width] = total[q * count:(q + 1) * count].astype(bf16)
        if ref.shape[1] > width:
            ref[:, width:] = both


def combine_body(half, *refs):
    shares, raw_ref, out_ref = refs[:half], refs[half], refs[-1]
    width = raw_ref.shape[1]
    update = shares[0][:, :width].astype(f32)
    for ref in shares[1:]:
        update = update + ref[:, :width].astype(f32)
    out_ref[...] = (raw_ref[...].astype(f32) + update).astype(bf16)


def merge_body(sections, layer_ref, *refs):
    blocks, tables = refs[:sections], refs[sections:2 * sections]
    state_ref, into_ref, held_ref, sems = refs[2 * sections:]
    layer = layer_ref[0]
    width = state_ref.shape[1]
    count = blocks[0].shape[0]
    routed = [ref[...].astype(f32) for ref in tables]
    shown = [row * jnp.where((layer ^ r) <= layer, 1.0, 0.0) for r, row in enumerate(routed)]
    select = []
    for r, rank in enumerate(ranked(routed)):
        later = jnp.zeros_like(rank)
        for other, row in enumerate(shown):
            if other != r:
                later = jnp.maximum(later, row * before(layer, r, other))
        select.append(selection(jnp.where(shown[r] > 0.5, rank * (1.0 - later), 0.0), count))
    select = stack_rows(select).astype(bf16)
    rows = stack_rows([block[...].astype(f32) for block in blocks]).astype(bf16)
    over = (((0,), (0,)), ((), ()))
    ones = jnp.ones((sections * count, LANES), bf16)
    hit = lax.dot_general(select, ones, over, preferred_element_type=f32)[:, :1]
    copies = []
    chunks = sems.shape[0]
    step = width // chunks
    for i in range(chunks):
        part = slice(i * step, (i + 1) * step)
        fresh = lax.dot_general(select, rows[:, part], over, preferred_element_type=f32)
        held_ref[:, part] = jnp.where(hit > 0.5, fresh.astype(bf16), state_ref[:, part])
        copies.append(pltpu.make_async_copy(held_ref.at[:, part], into_ref.at[:, part], sems.at[i]))
        copies[-1].start()
    for copy in copies:
        copy.wait()


def gram_body(scale, width, member_ref, mine_ref, far_ref, *refs):
    others, (out_ref, held_ref, sem) = refs[:-3], refs[-3:]
    member = member_ref[0] % GROUP
    mine = mine_ref[...]
    size, units = mine.shape
    theirs = far_ref[:, width:]
    blocks = [mine, stack_rows([theirs[:, :units].astype(f32), theirs[:, units:].astype(f32)]).astype(bf16)]
    for ref in others:
        both = spread(ref[:, width:].astype(f32), units).astype(bf16)
        blocks += [both[:size], both[size:]]
    for r, block in enumerate(blocks):
        term = scale * lax.dot_general(
            mine, block, (((0,), (0,)), ((), ())), preferred_element_type=f32
        )
        held_ref[:, pl.ds(pl.multiple_of((member ^ r) * units, units), units)] = term
    copy = pltpu.make_async_copy(held_ref, out_ref, sem)
    copy.start()
    copy.wait()


def passed(value, axis, r):
    return lax.ppermute(value, axis, [(i, i ^ r) for i in range(lax.axis_size(axis))])


def exchanged(value, axis):
    return [value] + [passed(value, axis, r) for r in range(1, lax.axis_size(axis))]


def shards(stream_in, gain, w_gate, w_up, w_down, routes, gates):
    fronts, tok_rows, width = stream_in.shape
    units = w_gate.shape[2]
    sections = lax.axis_size("layer")
    devices = lax.axis_size("expert")
    flight = devices // GROUP
    half = devices // 2
    tokens = fronts * tok_rows
    few = FEW * flight
    shape = jax.ShapeDtypeStruct
    layer = lax.axis_index("layer").astype(jnp.int32).reshape(1)
    member = lax.axis_index("expert").astype(jnp.int32).reshape(1)
    index = jnp.concatenate([layer, member])
    state = stream_in.reshape(tokens, width)
    routes = jnp.swapaxes(routes[0], 1, 2)
    gates = jnp.swapaxes(gates[0], 1, 2)
    w_gate, w_up, w_down = w_gate[0], w_up[0], w_down[0]
    scale = 1.0 / (fronts * CAP)
    mib = 2**20
    chunks = next(c for c in (7, 8, 4, 2, 1) if width % (c * LANES) == 0)

    def payload_of(count, raw, gate_weights):
        return call(
            functools.partial(meta_body, few),
            shape((count, width + LANES), bf16),
            sections + 2,
            scalars=1,
            limit=8 * mib,
        )(index, *tables, gate_weights, raw)

    def pass_shapes(size, wanted):
        return (
            shape((wanted, width), bf16),
            shape((wanted, width + LANES), bf16),
            shape((1, size), f32),
        )

    def pass_limit(size):
        return 8 * mib + 12 * size * width + 32 * size * size

    def summed(part, chosen):
        bits = [1 << b for b in range(devices.bit_length() - 1)]
        for bit in bits[:-1]:
            part = call(added_body, shape(part.shape, bf16), 2, traffic=6 * part.size)(
                part, passed(part, "expert", bit)
            )
        changed = call(
            changed_body, shape(chosen.shape, bf16), 3, traffic=8 * chosen.size, limit=2 * mib + 32 * chosen.size
        )(part, passed(part, "expert", bits[-1]), chosen)
        return exchanged(changed, "layer")

    def apply_limit(size, wanted):
        return 8 * mib + 16 * sections * wanted * width + 8 * size * width

    def applied(rows, sent, changed):
        size, wanted = rows.shape[0], changed[0].shape[0]
        return call(
            functools.partial(apply_body, sections),
            (shape(rows.shape, bf16), shape((1, 1), f32)),
            2 + sections,
            scalars=1,
            flops=2 * size * sections * wanted * width,
            traffic=4 * size * width,
            limit=apply_limit(size, wanted),
        )(layer, rows, sent, *changed)

    def passes(rows, count, weights):
        size = devices * count
        wanted = 2 * count
        part, chosen, sent = call(
            functools.partial(pass_body, count, flight),
            pass_shapes(size, wanted),
            5,
            scalars=1,
            flops=6 * wanted * width * units,
            traffic=2 * size * width,
            limit=pass_limit(size),
        )(member, rows, gain, *weights)
        return applied(rows, sent, summed(part, chosen))

    def finish(rows, count, weights, sent=None, changed=()):
        size = devices * count
        side = size // 2
        body = functools.partial(final_body, half, flight)
        operands = (member, rows)
        more_scratch = []
        if changed:
            body = functools.partial(changed_final_body, half, sections, flight)
            operands = (layer, member, rows, sent, *changed)
            more_scratch = [pltpu.VMEM(rows.shape, bf16), pltpu.VMEM((1, 1), f32)]
        hidden, raw, near, far = call(
            body,
            (
                shape((size, units), bf16),
                shape((count, width), bf16),
                shape((side, width), bf16),
                shape((side, width + 2 * units), bf16),
            ),
            5 + (1 + sections if changed else 0),
            scalars=2 if changed else 1,
            scratch=[pltpu.VMEM((devices, -(-count // 8) * 8, units), f32)] + more_scratch,
            flops=6 * size * width * units,
            traffic=6 * width * units,
            limit=8 * mib
            + 24 * min(size, CHUNK) * width
            + 4 * size * width
            + 16 * size * units
            + (apply_limit(size, changed[0].shape[0]) if changed else 0),
        )(*operands, gain, *weights)
        far = passed(far, "expert", 1)
        behind = 2 * devices * units
        sums = call(
            functools.partial(paired_body, half),
            tuple(
                shape((count, width + (behind if 0 < q < GROUP // 2 else 0)), bf16) for q in range(half)
            ),
            3,
            traffic=6 * side * width,
            limit=4 * mib + 20 * side * width + 24 * count * behind,
        )(near, far, hidden)
        arrived = [passed(sums[q], "expert", 2 * q) for q in range(half - 1, 0, -1)]
        arrived = [sums[0]] + arrived[::-1]
        fresh = call(
            functools.partial(combine_body, half),
            shape((count, width), bf16),
            half + 1,
            traffic=2 * side * width,
            limit=2 * mib + 16 * count * width + 6 * count * behind,
        )(*arrived, raw)
        blocks = exchanged(fresh, "layer")
        gram = call(
            functools.partial(gram_body, scale, width),
            shape((units, GROUP * units), f32),
            2 + GROUP // 2 - 1,
            scalars=1,
            scratch=[pltpu.VMEM((units, GROUP * units), f32), pltpu.SemaphoreType.DMA(())],
            placed=HBM,
            flops=2 * size * units * units * GROUP,
            traffic=4 * units * units * GROUP,
            limit=8 * mib + 64 * size * units,
        )(member, hidden, far, *arrived[1:GROUP // 2])
        new_state = call(
            functools.partial(merge_body, sections),
            shape((tokens, width), bf16),
            2 * sections + 1,
            scalars=1,
            scratch=[pltpu.VMEM((tokens, width), bf16), pltpu.SemaphoreType.DMA((chunks,))],
            placed=HBM,
            traffic=4 * tokens * width,
            limit=8 * mib + 16 * sections * count * width,
        )(layer, *blocks, *tables, state)
        return new_state, gram

    def looped(rows, more, count, weights):
        _, rows = lax.while_loop(
            lambda carry: carry[0][0, 0] > 0.5,
            lambda carry: passes(carry[1], count, weights)[::-1],
            (more, rows),
        )
        return finish(rows, count, weights)

    table, kept_routes = call(
        functools.partial(table_body, flight), (shape((1, tokens), bf16), shape(routes.shape, routes.dtype)), 1
    )(routes)
    tables = exchanged(table, "layer")
    raw = call(
        rows_body, shape((few, width), bf16), 2, traffic=2 * tokens * width, limit=8 * mib
    )(table, state)
    gate_weights = call(gates_body, shape((flight, tokens), f32), 2)(kept_routes, gates)
    payload = payload_of(few, raw, gate_weights)
    near = [payload] + [passed(payload, "expert", r) for r in range(2, devices, 2)]
    pair = passed(jnp.stack(near), "expert", 1)
    weights = call(
        held_body,
        tuple(shape(w.shape, bf16) for w in (w_gate, w_up, w_down)),
        1,
        streamed=3,
        scratch=[pltpu.SemaphoreType.DMA((3,))],
        traffic=12 * w_gate.size,
        limit=6 * w_gate.size + 2 * mib,
    )(near[1], w_gate, w_up, w_down)
    size = devices * few
    rows, mode, part, chosen, sent = call(
        functools.partial(first_pass_body, half, sections, few, flight),
        (shape((size, width + LANES), bf16), shape((1, 1), jnp.int32)) + pass_shapes(size, 2 * few),
        half + 5,
        scalars=1,
        flops=12 * few * width * units,
        traffic=4 * size * width,
        limit=pass_limit(size),
    )(member, *near, pair, gain, *weights)

    def once(share):
        def run(rows, part, chosen, sent, gate_weights, *weights):
            wanted = part.shape[0] // share
            return finish(rows, few, weights, sent, summed(part[:wanted], chosen[:wanted]))

        return run

    def again(rows, part, chosen, sent, gate_weights, *weights):
        rows, more = applied(rows, sent, summed(part, chosen))
        return looped(rows, more, few, weights)

    def filled(rows, part, chosen, sent, gate_weights, *weights):
        most = fronts * CAP * flight
        raw = call(
            rows_body, shape((most, width), bf16), 2, traffic=2 * tokens * width, limit=8 * mib
        )(table, state)
        payload = payload_of(most, raw, gate_weights)
        near = [payload] + [passed(payload, "expert", r) for r in range(2, devices, 2)]
        rows = call(
            functools.partial(stack_body, half),
            shape((devices * most, width + LANES), bf16),
            half + 1,
            traffic=4 * devices * most * width,
            limit=4 * mib + 16 * devices * most * width,
        )(*near, passed(jnp.stack(near), "expert", 1))
        return looped(rows, jnp.ones((1, 1), f32), most, weights)

    state, gram = lax.switch(
        mode[0, 0], (once(4), once(2), once(1), again, filled), rows, part, chosen, sent, gate_weights, *weights
    )
    return state.reshape(1, fronts, tok_rows, width), gram[None]


def solution(mesh):
    return jax.shard_map(
        shards,
        mesh=mesh,
        in_specs=(
            P(None, "expert", None),
            P("layer", None),
            P("layer", None, "expert"),
            P("layer", None, "expert"),
            P("layer", "expert", None),
            P("layer", None, "expert", None),
            P("layer", None, "expert", None),
        ),
        out_specs=(P("layer", None, "expert", None), P("layer", "expert", None)),
        check_vma=False,
    )
```

```python
import functools

import jax
import jax.numpy as jnp
from jax import lax
from jax.experimental import pallas as pl
from jax.experimental.pallas import tpu as pltpu
from jax.sharding import PartitionSpec as P

GROUP = 8
CAP = 2
EPSILON = 1e-06
LANES = 128
CHUNK = 128

FEW = 4

STATUS, SOURCE_LAYER, SOURCE_SLOT, WANTED, FULL, DEEP, DEVICE, SLOT, MORE = range(9)
COUNTS = 16
GATES = 32
READY, WAITS = 1.0, 2.0

f32 = jnp.float32
bf16 = jnp.bfloat16
VMEM = pl.BlockSpec(memory_space=pltpu.VMEM)
SMEM = pl.BlockSpec(memory_space=pltpu.SMEM)
HBM = pl.BlockSpec(memory_space=pltpu.HBM)


def call(
    body, out_shape, n_in, scalars=0, scratch=(), flops=0, traffic=0, limit=2 * 2**20, streamed=0, placed=None
):
    return pl.pallas_call(
        body,
        out_shape=out_shape,
        in_specs=[SMEM] * scalars + [VMEM] * n_in + [HBM] * streamed,
        out_specs=placed or jax.tree.map(lambda s: VMEM, out_shape),
        scratch_shapes=list(scratch),
        compiler_params=pltpu.CompilerParams(vmem_limit_bytes=limit),
        cost_estimate=pl.CostEstimate(flops=flops, bytes_accessed=traffic, transcendentals=0),
    )


def iota(shape, dim):
    return lax.broadcasted_iota(jnp.int32, shape, dim)


def stack_rows(rows):
    return jnp.concatenate(rows, axis=0)


def lane_of(extra, number):
    return extra[:, number:number + 1]


def across(column):
    size = column.shape[0]
    same = iota((size, size), 0) == iota((size, size), 1)
    return jnp.sum(jnp.where(same, column, 0.0), axis=0, keepdims=True)


def ranked(rows):
    size = rows[0].shape[1]
    upto = (iota((size, size), 0) <= iota((size, size), 1)).astype(f32).astype(bf16)
    rank = jnp.dot(stack_rows(rows).astype(bf16), upto, preferred_element_type=f32)
    return [rank[r:r + 1] * row for r, row in enumerate(rows)]


def selection(rank, count):
    wanted = (iota((count, rank.shape[1]), 0) + 1).astype(f32)
    return jnp.where(rank == wanted, 1.0, 0.0)


def normalized(rows, gain):
    scale = lax.rsqrt(jnp.mean(rows * rows, axis=-1, keepdims=True) + EPSILON)
    return (rows * scale * gain).astype(bf16)


def by_front(routes_ref, of_front):
    return jnp.concatenate([of_front(f) for f in range(routes_ref.shape[0])], axis=1)


def table_body(flight, routes_ref, table_ref, kept_ref):
    kept_ref[...] = routes_ref[...]
    table_ref[...] = by_front(
        routes_ref,
        lambda f: jnp.max(jnp.where(routes_ref[f] < flight, 1.0, 0.0), axis=0, keepdims=True),
    ).astype(bf16)


def held_body(after_ref, *refs):
    count = len(refs) // 2
    sems = refs[-1]
    copies = [pltpu.make_async_copy(refs[i], refs[count + i], sems.at[i]) for i in range(count)]
    for copy in copies:
        copy.start()
    for copy in copies:
        copy.wait()


def rows_body(skip, table_ref, state_ref, raw_ref):
    select = selection(ranked([table_ref[...].astype(f32)])[0] - skip, raw_ref.shape[0])
    raw_ref[...] = jnp.dot(select.astype(bf16), state_ref[...], preferred_element_type=f32).astype(bf16)


def gates_body(routes_ref, gates_ref, weights_ref):
    weights_ref[...] = stack_rows([
        by_front(
            routes_ref,
            lambda f: jnp.sum(jnp.where(routes_ref[f] == expert, gates_ref[f], 0.0), axis=0, keepdims=True),
        )
        for expert in range(weights_ref.shape[0])
    ])


def before(layer, a, b):
    return jnp.where((layer ^ a) < (layer ^ b), 1.0, 0.0)


def between(layer, a, b, routed):
    total = jnp.zeros_like(routed[0])
    for r, row in enumerate(routed):
        if r not in (a, b):
            total = jnp.maximum(total, row * before(layer, a, r) * before(layer, r, b))
    return total


def number_of(layer, r, sections):
    return sum(jnp.where((layer ^ r) == other, float(other), 0.0) for other in range(sections))


def meta_body(few, skip, index_ref, *refs):
    tables, (gates_ref, raw_ref, payload_ref) = refs[:-3], refs[-3:]
    layer, member = index_ref[0], index_ref[1]
    count, width = raw_ref.shape
    routed = [ref[...].astype(f32) for ref in tables]
    ranks = ranked(routed)
    waits = source_layer = source_slot = wanted = jnp.zeros_like(routed[0])
    for r in range(1, len(routed)):
        source = routed[r] * before(layer, r, 0) * (1.0 - between(layer, r, 0, routed))
        waits = waits + source
        source_layer = source_layer + source * number_of(layer, r, len(routed))
        source_slot = source_slot + source * ranks[r]
        wanted = jnp.maximum(wanted, routed[r] * before(layer, 0, r))
    status = jnp.where(waits > 0.5, WAITS, READY)
    full = sum(jnp.where(rank > few, 1.0, 0.0) for rank in ranks)
    deep = jnp.where(sum(routed) > 2.5, 1.0, 0.0)
    counts = [jnp.zeros_like(deep) for _ in routed]
    for r, row in enumerate(routed):
        later = jnp.zeros_like(row)
        for other, other_row in enumerate(routed):
            if other != r:
                later = jnp.maximum(later, other_row * before(layer, r, other))
        for place in range(len(counts)):
            counts[place] = counts[place] + row * later * jnp.where((layer ^ r) == place, 1.0, 0.0)
    gates = gates_ref[...]
    high = gates.astype(bf16).astype(f32)
    named = {STATUS: status, SOURCE_LAYER: source_layer, SOURCE_SLOT: source_slot, WANTED: wanted}
    named.update({FULL: full, DEEP: deep})
    named.update({COUNTS + place: row for place, row in enumerate(counts)})
    for expert in range(gates.shape[0]):
        named[GATES + expert] = high[expert:expert + 1]
        named[GATES + gates.shape[0] + expert] = (gates - high)[expert:expert + 1]
    last = -(-(max(named) + 1) // 8) * 8
    empty = jnp.zeros_like(deep)
    table = [named.get(number, empty) for number in range(last)]
    table = stack_rows(table + [jnp.zeros((LANES - last, deep.shape[1]), f32)]).astype(bf16)
    select = selection(ranks[0] - skip, count)
    left = stack_rows([select, jnp.ones_like(select)]).astype(bf16)
    both = lax.dot_general(left, table, (((1,), (1,)), ((), ())), preferred_element_type=f32)
    lane = iota((count, LANES), 1)
    by_column = jnp.logical_or(lane == FULL, lane == DEEP)
    by_column = jnp.logical_or(by_column, jnp.logical_and(lane >= COUNTS, lane < GATES))
    extra = jnp.where(by_column, both[count:], both[:count])
    extra = jnp.where(lane == DEVICE, jnp.full((count, LANES), member + 1, jnp.int32).astype(f32), extra)
    extra = jnp.where(lane == SLOT, (iota((count, LANES), 0) + (1 + skip)).astype(f32), extra)
    payload_ref[:, :width] = raw_ref[...]
    payload_ref[:, width:] = extra.astype(bf16)


def distances(half):
    return [2 * q for q in range(half)] + [2 * q + 1 for q in range(half)]


def stack_body(half, *refs):
    near, pair_ref, rows_ref = refs[:half], refs[half], refs[half + 1]
    blocks = [ref[...] for ref in near] + [pair_ref[q] for q in range(half)]
    count = blocks[0].shape[0]
    if count % 16 == 0:
        for place, block in enumerate(blocks):
            rows_ref[place * count:(place + 1) * count] = block
    else:
        rows_ref[...] = stack_rows([block.astype(f32) for block in blocks]).astype(bf16)


def pair_body(*refs):
    out_ref = refs[-1]
    for q in range(out_ref.shape[0]):
        out_ref[q] = refs[q][...]


def more_stack_body(half, rows_ref, *refs):
    near, pair_ref, into_ref = refs[:half], refs[half], refs[half + 1]
    more = [ref[...] for ref in near] + [pair_ref[q] for q in range(half)]
    count = more[0].shape[0]
    if count % 16 == 0:
        for place, block in enumerate(more):
            into_ref[2 * place * count:(2 * place + 1) * count] = rows_ref[place * count:(place + 1) * count]
            into_ref[(2 * place + 1) * count:(2 * place + 2) * count] = block
        return
    rows = rows_ref[...].astype(f32)
    stacked = []
    for place, block in enumerate(more):
        stacked += [rows[place * count:(place + 1) * count], block.astype(f32)]
    into_ref[...] = stack_rows(stacked).astype(bf16)


def first_pass_body(half, sections, count, flight, member_ref, *refs):
    gathered, refs = refs[:half + 1], refs[half + 1:]
    gain_ref, gate_ref, up_ref, down_ref, rows_ref, mode_ref, part_ref, chosen_ref, sent_ref = refs
    stack_body(half, *gathered, rows_ref)
    pass_body(count, flight, member_ref, rows_ref, gain_ref, gate_ref, up_ref, down_ref, part_ref, chosen_ref, sent_ref)
    extra = rows_ref[:, gain_ref.shape[1]:].astype(f32)
    most = jnp.max(extra, axis=0, keepdims=True)
    total = jnp.sum(jnp.where(lane_of(extra, SLOT) == 1.0, extra, 0.0), axis=0, keepdims=True)
    total = jnp.max(total[:, COUNTS:COUNTS + sections], axis=1, keepdims=True)
    wanted_count = part_ref.shape[0]
    mode = jnp.where(total > wanted_count // 4, 1, 0) + jnp.where(total > wanted_count // 2, 1, 0)
    again = jnp.where(total > wanted_count // 2, 4, 3)
    again = jnp.where(total > wanted_count, again, jnp.where(lane_of(most, DEEP) > 0.5, again, mode))
    mode_ref[...] = jnp.where(lane_of(most, FULL) > 0.5, 5, again)


def activated(rows, gate_ref, up_ref):
    gate = jnp.dot(rows, gate_ref[...], preferred_element_type=f32)
    up = jnp.dot(rows, up_ref[...], preferred_element_type=f32)
    return gate / (1.0 + jnp.exp(-gate)) * up


def weight_of(extra, member, flight):
    lane = iota(extra.shape, 1)
    expert = member // GROUP
    mine = jnp.logical_or(lane == GATES + expert, lane == GATES + flight + expert)
    return jnp.sum(jnp.where(mine, extra, 0.0), axis=1, keepdims=True)


def pass_body(count, flight, member_ref, rows_ref, gain_ref, gate_ref, up_ref, down_ref, part_ref, chosen_ref, sent_ref):
    member = member_ref[0]
    width = gain_ref.shape[1]
    wanted_count = part_ref.shape[0]
    extra = rows_ref[:, width:].astype(f32)
    wanted = lane_of(extra, WANTED)
    eligible = jnp.where(lane_of(extra, STATUS) == READY, wanted, 0.0)
    number = lane_of(extra, DEVICE) * count + lane_of(extra, SLOT)
    upto = number <= across(number)
    rank = jnp.sum(jnp.where(upto, eligible, 0.0), axis=0, keepdims=True) * across(eligible)
    select = selection(rank, wanted_count)
    chosen = jnp.dot(select.astype(bf16), rows_ref[...], preferred_element_type=f32)
    taken = jnp.sum(select, axis=0, keepdims=True)
    more = jnp.max(across(wanted) - taken, axis=1, keepdims=True)
    sent_ref[...] = taken
    lanes = chosen[:, width:]
    lane = iota(lanes.shape, 1)
    chosen_ref[:, :width] = chosen[:, :width].astype(bf16)
    chosen_ref[:, width:] = jnp.where(lane == MORE, more, lanes).astype(bf16)
    weight = weight_of(lanes, member, flight)
    hidden = activated(normalized(chosen[:, :width], gain_ref[...]), gate_ref, up_ref)
    if flight > 1:
        hidden = jnp.where(weight > 0.0, hidden, 0.0)
    share = jnp.dot(hidden.astype(bf16), down_ref[...], preferred_element_type=f32) * weight
    part_ref[...] = share.astype(bf16)


def added_body(a_ref, b_ref, out_ref):
    out_ref[...] = (a_ref[...].astype(f32) + b_ref[...].astype(f32)).astype(bf16)


def changed_body(a_ref, b_ref, chosen_ref, out_ref):
    width = a_ref.shape[1]
    total = chosen_ref[:, :width].astype(f32) + a_ref[...].astype(f32) + b_ref[...].astype(f32)
    out_ref[:, :width] = total.astype(bf16)
    out_ref[:, width:] = chosen_ref[:, width:]


def by_chunks(size, run):
    if size <= CHUNK:
        run(slice(0, size))
        return

    @pl.loop(0, size // CHUNK)
    def _(i):
        run(pl.ds(pl.multiple_of(i * CHUNK, CHUNK), CHUNK))


def apply_body(sections, layer_ref, rows_ref, sent_ref, *refs):
    changed, into_ref, more_ref = refs[:sections], refs[sections], refs[sections + 1]
    layer = layer_ref[0]
    width = rows_ref.shape[1] - LANES
    names = [ref[:, width:].astype(f32) for ref in changed]
    fresh = stack_rows([ref[:, :width].astype(f32) for ref in changed[1:]]).astype(bf16)
    columns = [(across(lane_of(name, DEVICE)), across(lane_of(name, SLOT))) for name in names]
    more = names[0]
    for name in names[1:]:
        more = jnp.maximum(more, name)
    more_ref[...] = jnp.max(lane_of(more, MORE), axis=0, keepdims=True)
    size = rows_ref.shape[0]
    taken = sent_ref[...]

    def run(part):
        extra = rows_ref[part, width:].astype(f32)
        waits = jnp.where(lane_of(extra, STATUS) == WAITS, 1.0, 0.0)
        matches = []
        for r in range(1, sections):
            device, slot = columns[r]
            match = jnp.where(lane_of(extra, DEVICE) == device, waits, 0.0)
            match = match * jnp.where(lane_of(extra, SOURCE_SLOT) == slot, 1.0, 0.0)
            from_it = jnp.where(lane_of(extra, SOURCE_LAYER) == number_of(layer, r, sections), 1.0, 0.0)
            matches.append(match * from_it)
        match = jnp.concatenate(matches, axis=1)
        arrived = jnp.max(match, axis=1, keepdims=True)
        new = jnp.dot(match.astype(bf16), fresh, preferred_element_type=f32)
        old = rows_ref[part, :width].astype(f32)
        into_ref[part, :width] = jnp.where(arrived > 0.5, new, old).astype(bf16)
        lane = iota(extra.shape, 1)
        extra = jnp.where(jnp.logical_and(lane == STATUS, arrived > 0.5), READY, extra)
        if size <= CHUNK:
            own = iota((size, size), 0) == iota((size, size), 1)
            gone = jnp.sum(jnp.where(own, taken, 0.0), axis=1, keepdims=True)
        else:
            first = part.start
            row = iota((CHUNK, size), 0) + first == iota((CHUNK, size), 1)
            gone = jnp.sum(jnp.where(row, taken, 0.0), axis=1, keepdims=True)
        extra = jnp.where(jnp.logical_and(lane == WANTED, gone > 0.5), 0.0, extra)
        into_ref[part, width:] = extra.astype(bf16)

    by_chunks(size, run)


def changed_final_body(half, sections, flight, layer_ref, member_ref, rows_ref, sent_ref, *refs):
    changed, rest, scratch = refs[:sections], refs[sections:-2], refs[-2:]
    into_ref, more_ref = scratch
    apply_body(sections, layer_ref, rows_ref, sent_ref, *changed, into_ref, more_ref)
    final_body(half, flight, member_ref, into_ref, *rest)


def final_body(half, flight, member_ref, rows_ref, gain_ref, gate_ref, up_ref, down_ref, hidden_ref, raw_ref, near_ref, far_ref, ordered_ref):
    member = member_ref[0]
    width = gain_ref.shape[1]
    units = hidden_ref.shape[1]
    size = rows_ref.shape[0]
    side = size // 2
    count = raw_ref.shape[0]
    raw_ref[...] = rows_ref[:, :width].astype(f32)[:count].astype(bf16) if size <= CHUNK else rows_ref[:count, :width]
    hidden_rows = []

    def run(part, of_part=None):
        extra = rows_ref[part, width:].astype(f32)
        weight = weight_of(extra, member, flight)
        hidden = activated(normalized(rows_ref[part, :width].astype(f32), gain_ref[...]), gate_ref, up_ref)
        if flight > 1:
            hidden = jnp.where(weight > 0.0, hidden, 0.0)
        share = jnp.dot(hidden.astype(bf16), down_ref[...], preferred_element_type=f32) * weight
        return hidden, share.astype(bf16)

    if size <= CHUNK:
        hidden, share = run(slice(0, size))
        near_ref[...] = share[:side]
        far_ref[:, :width] = share[side:]
        for place, r in enumerate(distances(half)):
            ordered_ref[member ^ r, :count] = hidden[place * count:(place + 1) * count]
    else:
        blocks = CHUNK // count

        def half_run(first, into_ref, odd):
            @pl.loop(0, side // CHUNK)
            def _(i):
                at = pl.multiple_of(i * CHUNK, CHUNK)
                hidden, share = run(pl.ds(pl.multiple_of(first + at, CHUNK), CHUNK))
                into_ref[pl.ds(at, CHUNK), :width] = share
                for b in range(blocks):
                    ordered_ref[member ^ (2 * (i * blocks + b) + odd)] = hidden[b * count:(b + 1) * count]

        half_run(0, near_ref, 0)
        half_run(side, far_ref, 1)
    hidden_rows = stack_rows([ordered_ref[source, :count] for source in range(2 * half)]).astype(bf16)
    hidden_ref[...] = hidden_rows
    far_ref[:, width:width + units] = hidden_rows[:side]
    far_ref[:, width + units:] = hidden_rows[side:]


def regrouped(rows, count):
    return jnp.concatenate([rows[i:i + count] for i in range(0, rows.shape[0], count)], axis=1)


def spread(block, units):
    return stack_rows([block[:, i:i + units] for i in range(0, block.shape[1], units)])


def paired_body(half, near_ref, far_ref, hidden_ref, *out_refs):
    width = near_ref.shape[1]
    units = hidden_ref.shape[1]
    count = near_ref.shape[0] // half
    total = near_ref[...].astype(f32) + far_ref[:, :width].astype(f32)
    theirs = far_ref[:, width:].astype(f32)
    both = [hidden_ref[...].astype(f32), theirs[:, :units], theirs[:, units:]]
    both = jnp.concatenate([regrouped(rows, count) for rows in both], axis=1).astype(bf16)
    for q, ref in enumerate(out_refs):
        ref[:, :width] = total[q * count:(q + 1) * count].astype(bf16)
        if ref.shape[1] > width:
            ref[:, width:] = both


def combine_body(half, *refs):
    shares, raw_ref, out_ref = refs[:half], refs[half], refs[-1]
    width = raw_ref.shape[1]
    update = shares[0][:, :width].astype(f32)
    for ref in shares[1:]:
        update = update + ref[:, :width].astype(f32)
    out_ref[...] = (raw_ref[...].astype(f32) + update).astype(bf16)


def merge_body(sections, layer_ref, *refs):
    blocks, tables = refs[:sections], refs[sections:2 * sections]
    state_ref, into_ref, held_ref, sems = refs[2 * sections:]
    layer = layer_ref[0]
    width = state_ref.shape[1]
    count = blocks[0].shape[0]
    routed = [ref[...].astype(f32) for ref in tables]
    shown = [row * jnp.where((layer ^ r) <= layer, 1.0, 0.0) for r, row in enumerate(routed)]
    select = []
    for r, rank in enumerate(ranked(routed)):
        later = jnp.zeros_like(rank)
        for other, row in enumerate(shown):
            if other != r:
                later = jnp.maximum(later, row * before(layer, r, other))
        select.append(selection(jnp.where(shown[r] > 0.5, rank * (1.0 - later), 0.0), count))
    select = stack_rows(select).astype(bf16)
    rows = stack_rows([block[...].astype(f32) for block in blocks]).astype(bf16)
    over = (((0,), (0,)), ((), ()))
    ones = jnp.ones((sections * count, LANES), bf16)
    hit = lax.dot_general(select, ones, over, preferred_element_type=f32)[:, :1]
    copies = []
    chunks = sems.shape[0]
    step = width // chunks
    for i in range(chunks):
        part = slice(i * step, (i + 1) * step)
        fresh = lax.dot_general(select, rows[:, part], over, preferred_element_type=f32)
        held_ref[:, part] = jnp.where(hit > 0.5, fresh.astype(bf16), state_ref[:, part])
        copies.append(pltpu.make_async_copy(held_ref.at[:, part], into_ref.at[:, part], sems.at[i]))
        copies[-1].start()
    for copy in copies:
        copy.wait()


def gram_body(scale, width, member_ref, mine_ref, far_ref, *refs):
    others, (out_ref, held_ref, sem) = refs[:-3], refs[-3:]
    member = member_ref[0] % GROUP
    mine = mine_ref[...]
    size, units = mine.shape
    theirs = far_ref[:, width:]
    blocks = [mine, stack_rows([theirs[:, :units].astype(f32), theirs[:, units:].astype(f32)]).astype(bf16)]
    for ref in others:
        both = spread(ref[:, width:].astype(f32), units).astype(bf16)
        blocks += [both[:size], both[size:]]
    for r, block in enumerate(blocks):
        term = scale * lax.dot_general(
            mine, block, (((0,), (0,)), ((), ())), preferred_element_type=f32
        )
        held_ref[:, pl.ds(pl.multiple_of((member ^ r) * units, units), units)] = term
    copy = pltpu.make_async_copy(held_ref, out_ref, sem)
    copy.start()
    copy.wait()


def passed(value, axis, r):
    return lax.ppermute(value, axis, [(i, i ^ r) for i in range(lax.axis_size(axis))])


def exchanged(value, axis):
    return [value] + [passed(value, axis, r) for r in range(1, lax.axis_size(axis))]


def shards(stream_in, gain, w_gate, w_up, w_down, routes, gates):
    fronts, tok_rows, width = stream_in.shape
    units = w_gate.shape[2]
    sections = lax.axis_size("layer")
    devices = lax.axis_size("expert")
    flight = devices // GROUP
    half = devices // 2
    tokens = fronts * tok_rows
    few = FEW * flight
    shape = jax.ShapeDtypeStruct
    layer = lax.axis_index("layer").astype(jnp.int32).reshape(1)
    member = lax.axis_index("expert").astype(jnp.int32).reshape(1)
    index = jnp.concatenate([layer, member])
    state = stream_in.reshape(tokens, width)
    routes = jnp.swapaxes(routes[0], 1, 2)
    gates = jnp.swapaxes(gates[0], 1, 2)
    w_gate, w_up, w_down = w_gate[0], w_up[0], w_down[0]
    scale = 1.0 / (fronts * CAP)
    mib = 2**20
    chunks = next(c for c in (7, 8, 4, 2, 1) if width % (c * LANES) == 0)

    def raw_of(count, skip):
        return call(
            functools.partial(rows_body, skip),
            shape((count, width), bf16),
            2,
            traffic=2 * tokens * width,
            limit=8 * mib,
        )(table, state)

    def payload_of(raw, gate_weights, skip):
        count = raw.shape[0]
        return call(
            functools.partial(meta_body, few, skip),
            shape((count, width + LANES), bf16),
            sections + 2,
            scalars=1,
            limit=8 * mib,
        )(index, *tables, gate_weights, raw)

    def near_of(payload):
        return [payload] + [passed(payload, "expert", r) for r in range(2, devices, 2)]

    def pair_of(near, after=()):
        count = near[0].shape[0]
        stacked = call(
            pair_body,
            shape((half, *near[0].shape), bf16),
            half + len(after),
            traffic=4 * half * count * width,
            limit=4 * mib + 8 * half * count * width,
        )(*near, *after)
        return passed(stacked, "expert", 1)

    def held(after, *weights):
        return call(
            held_body,
            tuple(shape(w.shape, bf16) for w in weights),
            1,
            streamed=len(weights),
            scratch=[pltpu.SemaphoreType.DMA((len(weights),))],
            traffic=4 * sum(w.size for w in weights),
            limit=2 * sum(w.size for w in weights) + 2 * mib,
        )(after, *weights)

    def pass_shapes(size, wanted):
        return (
            shape((wanted, width), bf16),
            shape((wanted, width + LANES), bf16),
            shape((1, size), f32),
        )

    def pass_limit(size):
        return 8 * mib + 12 * size * width + 32 * size * size

    def summed(part, chosen):
        bits = [1 << b for b in range(devices.bit_length() - 1)]
        for bit in bits[:-1]:
            part = call(added_body, shape(part.shape, bf16), 2, traffic=6 * part.size)(
                part, passed(part, "expert", bit)
            )
        changed = call(
            changed_body, shape(chosen.shape, bf16), 3, traffic=8 * chosen.size, limit=2 * mib + 32 * chosen.size
        )(part, passed(part, "expert", bits[-1]), chosen)
        return exchanged(changed, "layer")

    def apply_limit(size, wanted):
        return 8 * mib + 16 * sections * wanted * width + 8 * size * width

    def applied(rows, sent, changed):
        size, wanted = rows.shape[0], changed[0].shape[0]
        return call(
            functools.partial(apply_body, sections),
            (shape(rows.shape, bf16), shape((1, 1), f32)),
            2 + sections,
            scalars=1,
            flops=2 * size * sections * wanted * width,
            traffic=4 * size * width,
            limit=apply_limit(size, wanted),
        )(layer, rows, sent, *changed)

    def passes(rows, wanted, weights):
        size = rows.shape[0]
        count = size // devices
        part, chosen, sent = call(
            functools.partial(pass_body, count, flight),
            pass_shapes(size, wanted),
            5,
            scalars=1,
            flops=6 * wanted * width * units,
            traffic=2 * size * width,
            limit=pass_limit(size),
        )(member, rows, gain, *weights)
        return applied(rows, sent, summed(part, chosen))

    def finish(rows, count, weights, sent=None, changed=()):
        size = devices * count
        side = size // 2
        body = functools.partial(final_body, half, flight)
        operands = (member, rows)
        more_scratch = []
        if changed:
            body = functools.partial(changed_final_body, half, sections, flight)
            operands = (layer, member, rows, sent, *changed)
            more_scratch = [pltpu.VMEM(rows.shape, bf16), pltpu.VMEM((1, 1), f32)]
        hidden, raw, near, far = call(
            body,
            (
                shape((size, units), bf16),
                shape((count, width), bf16),
                shape((side, width), bf16),
                shape((side, width + 2 * units), bf16),
            ),
            5 + (1 + sections if changed else 0),
            scalars=2 if changed else 1,
            scratch=[pltpu.VMEM((devices, -(-count // 8) * 8, units), f32)] + more_scratch,
            flops=6 * size * width * units,
            traffic=6 * width * units,
            limit=8 * mib
            + 24 * min(size, CHUNK) * width
            + 4 * size * width
            + 16 * size * units
            + (apply_limit(size, changed[0].shape[0]) if changed else 0),
        )(*operands, gain, *weights)
        far = passed(far, "expert", 1)
        behind = 2 * devices * units
        sums = call(
            functools.partial(paired_body, half),
            tuple(
                shape((count, width + (behind if 0 < q < GROUP // 2 else 0)), bf16) for q in range(half)
            ),
            3,
            traffic=6 * side * width,
            limit=4 * mib + 20 * side * width + 24 * count * behind,
        )(near, far, hidden)
        arrived = [passed(sums[q], "expert", 2 * q) for q in range(half - 1, 0, -1)]
        arrived = [sums[0]] + arrived[::-1]
        fresh = call(
            functools.partial(combine_body, half),
            shape((count, width), bf16),
            half + 1,
            traffic=2 * side * width,
            limit=2 * mib + 16 * count * width + 6 * count * behind,
        )(*arrived, raw)
        blocks = exchanged(fresh, "layer")
        gram = call(
            functools.partial(gram_body, scale, width),
            shape((units, GROUP * units), f32),
            2 + GROUP // 2 - 1,
            scalars=1,
            scratch=[pltpu.VMEM((units, GROUP * units), f32), pltpu.SemaphoreType.DMA(())],
            placed=HBM,
            flops=2 * size * units * units * GROUP,
            traffic=4 * units * units * GROUP,
            limit=8 * mib + 64 * size * units,
        )(member, hidden, far, *arrived[1:GROUP // 2])
        new_state = call(
            functools.partial(merge_body, sections),
            shape((tokens, width), bf16),
            2 * sections + 1,
            scalars=1,
            scratch=[pltpu.VMEM((tokens, width), bf16), pltpu.SemaphoreType.DMA((chunks,))],
            placed=HBM,
            traffic=4 * tokens * width,
            limit=8 * mib + 16 * sections * count * width,
        )(layer, *blocks, *tables, state)
        return new_state, gram

    def looped(rows, more, weights):
        _, rows = lax.while_loop(
            lambda carry: carry[0][0, 0] > 0.5,
            lambda carry: passes(carry[1], few, weights)[::-1],
            (more, rows),
        )
        return finish(rows, rows.shape[0] // devices, weights)

    table, kept_routes = call(
        functools.partial(table_body, flight), (shape((1, tokens), bf16), shape(routes.shape, routes.dtype)), 1
    )(routes)
    tables = exchanged(table, "layer")
    raw = raw_of(few, 0)
    gate_weights = call(gates_body, shape((flight, tokens), f32), 2)(kept_routes, gates)
    payload = payload_of(raw, gate_weights, 0)
    near = near_of(payload)
    early = held(payload, w_gate)
    pair = pair_of(near, early)
    weights = *early, *held(near[1], w_up, w_down)
    size = devices * few
    rows, mode, part, chosen, sent = call(
        functools.partial(first_pass_body, half, sections, few, flight),
        (shape((size, width + LANES), bf16), shape((1, 1), jnp.int32)) + pass_shapes(size, 2 * few),
        half + 5,
        scalars=1,
        flops=12 * few * width * units,
        traffic=4 * size * width,
        limit=pass_limit(size),
    )(member, *near, pair, gain, *weights)

    def once(share):
        def run(rows, part, chosen, sent, gate_weights, *weights):
            wanted = part.shape[0] // share
            return finish(rows, few, weights, sent, summed(part[:wanted], chosen[:wanted]))

        return run

    def again(share):
        def run(rows, part, chosen, sent, gate_weights, *weights):
            wanted = part.shape[0] // share
            rows, more = applied(rows, sent, summed(part[:wanted], chosen[:wanted]))
            return looped(rows, more, weights)

        return run

    def filled(rows, part, chosen, sent, gate_weights, *weights):
        most = fronts * CAP * flight
        near = near_of(payload_of(raw_of(most - few, few), gate_weights, few))
        rows = call(
            functools.partial(more_stack_body, half),
            shape((devices * most, width + LANES), bf16),
            half + 2,
            traffic=4 * devices * most * width,
            limit=4 * mib + 16 * devices * most * width,
        )(rows, *near, pair_of(near))
        rows, more = passes(rows, 4 * few, weights)
        return looped(rows, more, weights)

    state, gram = lax.switch(
        mode[0, 0], (once(4), once(2), once(1), again(2), again(1), filled), rows, part, chosen, sent, gate_weights, *weights
    )
    return state.reshape(1, fronts, tok_rows, width), gram[None]


def solution(mesh):
    return jax.shard_map(
        shards,
        mesh=mesh,
        in_specs=(
            P(None, "expert", None),
            P("layer", None),
            P("layer", None, "expert"),
            P("layer", None, "expert"),
            P("layer", "expert", None),
            P("layer", None, "expert", None),
            P("layer", None, "expert", None),
        ),
        out_specs=(P("layer", None, "expert", None), P("layer", "expert", None)),
        check_vma=False,
    )
```

```python
import functools

import jax
import jax.numpy as jnp
from jax import lax
from jax.experimental import pallas as pl
from jax.experimental.pallas import tpu as pltpu
from jax.sharding import PartitionSpec as P

GROUP = 8
CAP = 2
EPSILON = 1e-06
LANES = 128
CHUNK = 128

FEW = 4

STATUS, SOURCE_LAYER, SOURCE_SLOT, WANTED, FULL, DEEP, DEVICE, SLOT, MORE = range(9)
COUNTS = 16
GATES = 32
READY, WAITS = 1.0, 2.0

f32 = jnp.float32
bf16 = jnp.bfloat16
VMEM = pl.BlockSpec(memory_space=pltpu.VMEM)
HBM = pl.BlockSpec(memory_space=pltpu.HBM)


def whereabouts():
    return lax.axis_index("layer").astype(jnp.int32), lax.axis_index("expert").astype(jnp.int32)


def call(
    body, out_shape, n_in, scratch=(), flops=0, traffic=0, limit=2 * 2**20, streamed=0, placed=None
):
    return pl.pallas_call(
        body,
        out_shape=out_shape,
        in_specs=[VMEM] * n_in + [HBM] * streamed,
        out_specs=placed or jax.tree.map(lambda s: VMEM, out_shape),
        scratch_shapes=list(scratch),
        compiler_params=pltpu.CompilerParams(vmem_limit_bytes=limit),
        cost_estimate=pl.CostEstimate(flops=flops, bytes_accessed=traffic, transcendentals=0),
    )


def iota(shape, dim):
    return lax.broadcasted_iota(jnp.int32, shape, dim)


def stack_rows(rows):
    return jnp.concatenate(rows, axis=0)


def lane_of(extra, number):
    return extra[:, number:number + 1]


def across(column):
    size = column.shape[0]
    same = iota((size, size), 0) == iota((size, size), 1)
    return jnp.sum(jnp.where(same, column, 0.0), axis=0, keepdims=True)


def ranked(rows):
    size = rows[0].shape[1]
    upto = (iota((size, size), 0) <= iota((size, size), 1)).astype(f32).astype(bf16)
    rank = jnp.dot(stack_rows(rows).astype(bf16), upto, preferred_element_type=f32)
    return [rank[r:r + 1] * row for r, row in enumerate(rows)]


def selection(rank, count):
    wanted = (iota((count, rank.shape[1]), 0) + 1).astype(f32)
    return jnp.where(rank == wanted, 1.0, 0.0)


def normalized(rows, gain):
    scale = lax.rsqrt(jnp.mean(rows * rows, axis=-1, keepdims=True) + EPSILON)
    return (rows * scale * gain).astype(bf16)


def by_front(routes_ref, of_front):
    return jnp.concatenate([of_front(f) for f in range(routes_ref.shape[0])], axis=1)


def table_body(flight, routes_ref, table_ref, kept_ref):
    kept_ref[...] = routes_ref[...]
    table_ref[...] = by_front(
        routes_ref,
        lambda f: jnp.max(jnp.where(routes_ref[f] < flight, 1.0, 0.0), axis=0, keepdims=True),
    ).astype(bf16)


def held_body(after_ref, *refs):
    count = len(refs) // 2
    sems = refs[-1]
    copies = [pltpu.make_async_copy(refs[i], refs[count + i], sems.at[i]) for i in range(count)]
    for copy in copies:
        copy.start()
    for copy in copies:
        copy.wait()


def rows_body(skip, table_ref, state_ref, raw_ref):
    select = selection(ranked([table_ref[...].astype(f32)])[0] - skip, raw_ref.shape[0])
    raw_ref[...] = jnp.dot(select.astype(bf16), state_ref[...], preferred_element_type=f32).astype(bf16)


def gates_body(routes_ref, gates_ref, weights_ref):
    weights_ref[...] = stack_rows([
        by_front(
            routes_ref,
            lambda f: jnp.sum(jnp.where(routes_ref[f] == expert, gates_ref[f], 0.0), axis=0, keepdims=True),
        )
        for expert in range(weights_ref.shape[0])
    ])


def before(layer, a, b):
    return jnp.where((layer ^ a) < (layer ^ b), 1.0, 0.0)


def between(layer, a, b, routed):
    total = jnp.zeros_like(routed[0])
    for r, row in enumerate(routed):
        if r not in (a, b):
            total = jnp.maximum(total, row * before(layer, a, r) * before(layer, r, b))
    return total


def number_of(layer, r, sections):
    return sum(jnp.where((layer ^ r) == other, float(other), 0.0) for other in range(sections))


def meta_body(few, skip, *refs):
    tables, (gates_ref, raw_ref, payload_ref) = refs[:-3], refs[-3:]
    layer, member = whereabouts()
    count, width = raw_ref.shape
    routed = [ref[...].astype(f32) for ref in tables]
    ranks = ranked(routed)
    waits = source_layer = source_slot = wanted = jnp.zeros_like(routed[0])
    for r in range(1, len(routed)):
        source = routed[r] * before(layer, r, 0) * (1.0 - between(layer, r, 0, routed))
        waits = waits + source
        source_layer = source_layer + source * number_of(layer, r, len(routed))
        source_slot = source_slot + source * ranks[r]
        wanted = jnp.maximum(wanted, routed[r] * before(layer, 0, r))
    status = jnp.where(waits > 0.5, WAITS, READY)
    full = sum(jnp.where(rank > few, 1.0, 0.0) for rank in ranks)
    deep = jnp.where(sum(routed) > 2.5, 1.0, 0.0)
    counts = [jnp.zeros_like(deep) for _ in routed]
    for r, row in enumerate(routed):
        later = jnp.zeros_like(row)
        for other, other_row in enumerate(routed):
            if other != r:
                later = jnp.maximum(later, other_row * before(layer, r, other))
        for place in range(len(counts)):
            counts[place] = counts[place] + row * later * jnp.where((layer ^ r) == place, 1.0, 0.0)
    gates = gates_ref[...]
    high = gates.astype(bf16).astype(f32)
    named = {STATUS: status, SOURCE_LAYER: source_layer, SOURCE_SLOT: source_slot, WANTED: wanted}
    named.update({FULL: full, DEEP: deep})
    named.update({COUNTS + place: row for place, row in enumerate(counts)})
    for expert in range(gates.shape[0]):
        named[GATES + expert] = high[expert:expert + 1]
        named[GATES + gates.shape[0] + expert] = (gates - high)[expert:expert + 1]
    last = -(-(max(named) + 1) // 8) * 8
    empty = jnp.zeros_like(deep)
    table = [named.get(number, empty) for number in range(last)]
    table = stack_rows(table + [jnp.zeros((LANES - last, deep.shape[1]), f32)]).astype(bf16)
    select = selection(ranks[0] - skip, count)
    left = stack_rows([select, jnp.ones_like(select)]).astype(bf16)
    both = lax.dot_general(left, table, (((1,), (1,)), ((), ())), preferred_element_type=f32)
    lane = iota((count, LANES), 1)
    by_column = jnp.logical_or(lane == FULL, lane == DEEP)
    by_column = jnp.logical_or(by_column, jnp.logical_and(lane >= COUNTS, lane < GATES))
    extra = jnp.where(by_column, both[count:], both[:count])
    extra = jnp.where(lane == DEVICE, jnp.full((count, LANES), member + 1, jnp.int32).astype(f32), extra)
    extra = jnp.where(lane == SLOT, (iota((count, LANES), 0) + (1 + skip)).astype(f32), extra)
    payload_ref[:, :width] = raw_ref[...]
    payload_ref[:, width:] = extra.astype(bf16)


def distances(half):
    return [2 * q for q in range(half)] + [2 * q + 1 for q in range(half)]


def parts_of(half):
    later = list(range(1, half // 2 + 1))
    return [q for q in range(half) if q not in later], later


def gathered_blocks(half, near, pairs):
    blocks = [ref[...] for ref in near]
    odd = {}
    for ref, part in zip(pairs, parts_of(half)):
        odd.update({q: ref[i] for i, q in enumerate(part)})
    return blocks + [odd[q] for q in range(half)]


def stack_body(half, *refs):
    rows_ref = refs[half + 2]
    blocks = gathered_blocks(half, refs[:half], refs[half:half + 2])
    count = blocks[0].shape[0]
    if count % 16 == 0:
        for place, block in enumerate(blocks):
            rows_ref[place * count:(place + 1) * count] = block
    else:
        rows_ref[...] = stack_rows([block.astype(f32) for block in blocks]).astype(bf16)


def pair_body(*refs):
    out_ref = refs[-1]
    for q in range(out_ref.shape[0]):
        out_ref[q] = refs[q][...]


def more_stack_body(half, rows_ref, *refs):
    into_ref = refs[half + 2]
    more = gathered_blocks(half, refs[:half], refs[half:half + 2])
    count = more[0].shape[0]
    if count % 16 == 0:
        for place, block in enumerate(more):
            into_ref[2 * place * count:(2 * place + 1) * count] = rows_ref[place * count:(place + 1) * count]
            into_ref[(2 * place + 1) * count:(2 * place + 2) * count] = block
        return
    rows = rows_ref[...].astype(f32)
    stacked = []
    for place, block in enumerate(more):
        stacked += [rows[place * count:(place + 1) * count], block.astype(f32)]
    into_ref[...] = stack_rows(stacked).astype(bf16)


def first_pass_body(half, sections, count, flight, *refs):
    gathered, refs = refs[:half + 2], refs[half + 2:]
    gain_ref, gate_ref, up_ref, down_ref, rows_ref, mode_ref, part_ref, chosen_ref, sent_ref = refs
    stack_body(half, *gathered, rows_ref)
    pass_body(count, flight, rows_ref, gain_ref, gate_ref, up_ref, down_ref, part_ref, chosen_ref, sent_ref)
    extra = rows_ref[:, gain_ref.shape[1]:].astype(f32)
    most = jnp.max(extra, axis=0, keepdims=True)
    total = jnp.sum(jnp.where(lane_of(extra, SLOT) == 1.0, extra, 0.0), axis=0, keepdims=True)
    total = jnp.max(total[:, COUNTS:COUNTS + sections], axis=1, keepdims=True)
    wanted_count = part_ref.shape[0]
    mode = jnp.where(total > wanted_count // 4, 1, 0) + jnp.where(total > wanted_count // 2, 1, 0)
    again = jnp.where(total > wanted_count // 2, 4, 3)
    again = jnp.where(total > wanted_count, again, jnp.where(lane_of(most, DEEP) > 0.5, again, mode))
    mode_ref[...] = jnp.where(lane_of(most, FULL) > 0.5, 5, again)


def activated(rows, gate_ref, up_ref):
    gate = jnp.dot(rows, gate_ref[...], preferred_element_type=f32)
    up = jnp.dot(rows, up_ref[...], preferred_element_type=f32)
    return gate / (1.0 + jnp.exp(-gate)) * up


def weight_of(extra, member, flight):
    lane = iota(extra.shape, 1)
    expert = member // GROUP
    mine = jnp.logical_or(lane == GATES + expert, lane == GATES + flight + expert)
    return jnp.sum(jnp.where(mine, extra, 0.0), axis=1, keepdims=True)


def pass_body(count, flight, rows_ref, gain_ref, gate_ref, up_ref, down_ref, part_ref, chosen_ref, sent_ref):
    member = whereabouts()[1]
    width = gain_ref.shape[1]
    wanted_count = part_ref.shape[0]
    extra = rows_ref[:, width:].astype(f32)
    wanted = lane_of(extra, WANTED)
    eligible = jnp.where(lane_of(extra, STATUS) == READY, wanted, 0.0)
    number = lane_of(extra, DEVICE) * count + lane_of(extra, SLOT)
    upto = number <= across(number)
    rank = jnp.sum(jnp.where(upto, eligible, 0.0), axis=0, keepdims=True) * across(eligible)
    select = selection(rank, wanted_count)
    chosen = jnp.dot(select.astype(bf16), rows_ref[...], preferred_element_type=f32)
    taken = jnp.sum(select, axis=0, keepdims=True)
    more = jnp.max(across(wanted) - taken, axis=1, keepdims=True)
    sent_ref[...] = taken
    lanes = chosen[:, width:]
    lane = iota(lanes.shape, 1)
    chosen_ref[:, :width] = chosen[:, :width].astype(bf16)
    chosen_ref[:, width:] = jnp.where(lane == MORE, more, lanes).astype(bf16)
    weight = weight_of(lanes, member, flight)
    hidden = activated(normalized(chosen[:, :width], gain_ref[...]), gate_ref, up_ref)
    if flight > 1:
        hidden = jnp.where(weight > 0.0, hidden, 0.0)
    share = jnp.dot(hidden.astype(bf16), down_ref[...], preferred_element_type=f32) * weight
    part_ref[...] = share.astype(bf16)


def added_body(a_ref, b_ref, out_ref):
    out_ref[...] = (a_ref[...].astype(f32) + b_ref[...].astype(f32)).astype(bf16)


def changed_body(a_ref, b_ref, chosen_ref, out_ref):
    width = a_ref.shape[1]
    total = chosen_ref[:, :width].astype(f32) + a_ref[...].astype(f32) + b_ref[...].astype(f32)
    out_ref[:, :width] = total.astype(bf16)
    out_ref[:, width:] = chosen_ref[:, width:]


def by_chunks(size, run):
    if size <= CHUNK:
        run(slice(0, size))
        return

    @pl.loop(0, size // CHUNK)
    def _(i):
        run(pl.ds(pl.multiple_of(i * CHUNK, CHUNK), CHUNK))


def apply_body(sections, rows_ref, sent_ref, *refs):
    changed, into_ref, more_ref = refs[:sections], refs[sections], refs[sections + 1]
    layer = whereabouts()[0]
    width = rows_ref.shape[1] - LANES
    names = [ref[:, width:].astype(f32) for ref in changed]
    fresh = stack_rows([ref[:, :width].astype(f32) for ref in changed[1:]]).astype(bf16)
    columns = [(across(lane_of(name, DEVICE)), across(lane_of(name, SLOT))) for name in names]
    more = names[0]
    for name in names[1:]:
        more = jnp.maximum(more, name)
    more_ref[...] = jnp.max(lane_of(more, MORE), axis=0, keepdims=True)
    size = rows_ref.shape[0]
    taken = sent_ref[...]

    def run(part):
        extra = rows_ref[part, width:].astype(f32)
        waits = jnp.where(lane_of(extra, STATUS) == WAITS, 1.0, 0.0)
        matches = []
        for r in range(1, sections):
            device, slot = columns[r]
            match = jnp.where(lane_of(extra, DEVICE) == device, waits, 0.0)
            match = match * jnp.where(lane_of(extra, SOURCE_SLOT) == slot, 1.0, 0.0)
            from_it = jnp.where(lane_of(extra, SOURCE_LAYER) == number_of(layer, r, sections), 1.0, 0.0)
            matches.append(match * from_it)
        match = jnp.concatenate(matches, axis=1)
        arrived = jnp.max(match, axis=1, keepdims=True)
        new = jnp.dot(match.astype(bf16), fresh, preferred_element_type=f32)
        old = rows_ref[part, :width].astype(f32)
        into_ref[part, :width] = jnp.where(arrived > 0.5, new, old).astype(bf16)
        lane = iota(extra.shape, 1)
        extra = jnp.where(jnp.logical_and(lane == STATUS, arrived > 0.5), READY, extra)
        if size <= CHUNK:
            own = iota((size, size), 0) == iota((size, size), 1)
            gone = jnp.sum(jnp.where(own, taken, 0.0), axis=1, keepdims=True)
        else:
            first = part.start
            row = iota((CHUNK, size), 0) + first == iota((CHUNK, size), 1)
            gone = jnp.sum(jnp.where(row, taken, 0.0), axis=1, keepdims=True)
        extra = jnp.where(jnp.logical_and(lane == WANTED, gone > 0.5), 0.0, extra)
        into_ref[part, width:] = extra.astype(bf16)

    by_chunks(size, run)


def changed_final_body(half, sections, flight, rows_ref, sent_ref, *refs):
    changed, rest, scratch = refs[:sections], refs[sections:-2], refs[-2:]
    into_ref, more_ref = scratch
    apply_body(sections, rows_ref, sent_ref, *changed, into_ref, more_ref)
    final_body(half, flight, into_ref, *rest)


def final_body(
    half, flight, rows_ref, gain_ref, gate_ref, up_ref, down_ref,
    hidden_ref, raw_ref, near_ref, soon_ref, late_ref, ordered_ref
):
    member = whereabouts()[1]
    width = gain_ref.shape[1]
    units = hidden_ref.shape[1]
    size = rows_ref.shape[0]
    side = size // 2
    count = raw_ref.shape[0]
    raw_ref[...] = rows_ref[:, :width].astype(f32)[:count].astype(bf16) if size <= CHUNK else rows_ref[:count, :width]
    hidden_rows = []

    def run(part, of_part=None):
        extra = rows_ref[part, width:].astype(f32)
        weight = weight_of(extra, member, flight)
        hidden = activated(normalized(rows_ref[part, :width].astype(f32), gain_ref[...]), gate_ref, up_ref)
        if flight > 1:
            hidden = jnp.where(weight > 0.0, hidden, 0.0)
        share = jnp.dot(hidden.astype(bf16), down_ref[...], preferred_element_type=f32) * weight
        return hidden, share

    if size <= CHUNK:
        hidden, share = run(slice(0, size))
        near_ref[...] = share[:side].astype(bf16)
        late_ref[...] = share[side:side + side // 2].astype(bf16)
        soon_ref[:, :width] = share[side + side // 2:].astype(bf16)
        for place, r in enumerate(distances(half)):
            ordered_ref[member ^ r, :count] = hidden[place * count:(place + 1) * count]
    else:
        blocks = CHUNK // count

        def part_run(first, size, into_ref, block, odd):
            @pl.loop(0, size // CHUNK)
            def _(i):
                at = pl.multiple_of(i * CHUNK, CHUNK)
                hidden, share = run(pl.ds(pl.multiple_of(first + at, CHUNK), CHUNK))
                into_ref[pl.ds(at, CHUNK), :width] = share.astype(bf16)
                for b in range(blocks):
                    distance = 2 * (block + i * blocks + b) + odd
                    ordered_ref[member ^ distance] = hidden[b * count:(b + 1) * count]

        part_run(0, side, near_ref, 0, 0)
        part_run(side, side // 2, late_ref, 0, 1)
        part_run(side + side // 2, side // 2, soon_ref, half // 2, 1)
    ordered_rows = stack_rows([ordered_ref[source, :count] for source in range(2 * half)])
    hidden_rows = ordered_rows.astype(bf16)
    hidden_ref[...] = hidden_rows
    quarter = side // 2
    for i in range(4):
        rows_of = slice(i * quarter, (i + 1) * quarter)
        values = ordered_rows[rows_of].astype(bf16) if quarter % 16 else hidden_rows[rows_of]
        soon_ref[:, width + i * units:width + (i + 1) * units] = values


def regrouped(rows, count):
    return jnp.concatenate([rows[i:i + count] for i in range(0, rows.shape[0], count)], axis=1)


def spread(block, units):
    return stack_rows([block[:, i:i + units] for i in range(0, block.shape[1], units)])


def their_hidden(soon_ref, width, units):
    behind = soon_ref[:, width:].astype(f32)
    return stack_rows([behind[:, i:i + units] for i in range(0, behind.shape[1], units)])


def paired_body(half, first, number, near_ref, far_ref, soon_ref, hidden_ref, *out_refs):
    width = near_ref.shape[1]
    units = hidden_ref.shape[1]
    count = near_ref.shape[0] // half
    mine = near_ref[...].astype(f32)[first * count:(first + number) * count]
    total = mine + far_ref[:, :width].astype(f32)
    both = None
    for q, ref in enumerate(out_refs):
        ref[:, :width] = total[q * count:(q + 1) * count].astype(bf16)
        if ref.shape[1] > width:
            if both is None:
                both = [hidden_ref[...].astype(f32), their_hidden(soon_ref, width, units)]
                both = jnp.concatenate([regrouped(rows, count) for rows in both], axis=1).astype(bf16)
            ref[:, width:] = both


def combine_body(half, *refs):
    shares, raw_ref, out_ref = refs[:half], refs[half], refs[-1]
    width = raw_ref.shape[1]
    update = shares[0][:, :width].astype(f32)
    for ref in shares[1:]:
        update = update + ref[:, :width].astype(f32)
    out_ref[...] = (raw_ref[...].astype(f32) + update).astype(bf16)


def plan_body(sections, count, *refs):
    tables = refs[:sections]
    state_ref, _, select_ref, base_ref = refs[sections:]
    layer = whereabouts()[0]
    routed = [ref[...].astype(f32) for ref in tables]
    shown = [row * jnp.where((layer ^ r) <= layer, 1.0, 0.0) for r, row in enumerate(routed)]
    select = []
    for r, rank in enumerate(ranked(routed)):
        later = jnp.zeros_like(rank)
        for other, row in enumerate(shown):
            if other != r:
                later = jnp.maximum(later, row * before(layer, r, other))
        select.append(selection(jnp.where(shown[r] > 0.5, rank * (1.0 - later), 0.0), count))
    select = stack_rows(select).astype(bf16)
    size = select.shape[0]
    same = (iota((size, size), 0) == iota((size, size), 1)).astype(f32).astype(bf16)
    over = (((0,), (0,)), ((), ()))
    turned = lax.dot_general(select, same, over, preferred_element_type=f32)
    select_ref[...] = turned.astype(bf16)
    hit = jnp.sum(turned, axis=1, keepdims=True)
    base_ref[...] = jnp.where(hit > 0.5, 0.0, state_ref[...].astype(f32)).astype(bf16)


def merge_body(sections, *refs):
    blocks = refs[:sections]
    select_ref, base_ref, into_ref, held_ref, sems = refs[sections:]
    width = base_ref.shape[1]
    rows = stack_rows([block[...].astype(f32) for block in blocks]).astype(bf16)
    copies = []
    chunks = sems.shape[0]
    step = width // chunks
    for i in range(chunks):
        part = slice(i * step, (i + 1) * step)
        fresh = jnp.dot(select_ref[...], rows[:, part], preferred_element_type=f32)
        held_ref[:, part] = (fresh + base_ref[:, part].astype(f32)).astype(bf16)
        copies.append(pltpu.make_async_copy(held_ref.at[:, part], into_ref.at[:, part], sems.at[i]))
        copies[-1].start()
    for copy in copies:
        copy.wait()


def gram_body(scale, width, mine_ref, far_ref, *refs):
    others, (out_ref, held_ref, sem) = refs[:-3], refs[-3:]
    member = whereabouts()[1] % GROUP
    mine = mine_ref[...]
    size, units = mine.shape
    blocks = [mine, their_hidden(far_ref, width, units).astype(bf16)]
    for ref in others:
        both = spread(ref[:, width:].astype(f32), units).astype(bf16)
        blocks += [both[:size], both[size:]]
    for r, block in enumerate(blocks):
        term = scale * lax.dot_general(
            mine, block, (((0,), (0,)), ((), ())), preferred_element_type=f32
        )
        held_ref[:, pl.ds(pl.multiple_of((member ^ r) * units, units), units)] = term
    copy = pltpu.make_async_copy(held_ref, out_ref, sem)
    copy.start()
    copy.wait()


def passed(value, axis, r):
    return lax.ppermute(value, axis, [(i, i ^ r) for i in range(lax.axis_size(axis))])


def exchanged(value, axis):
    return [value] + [passed(value, axis, r) for r in range(1, lax.axis_size(axis))]


def shards(stream_in, gain, w_gate, w_up, w_down, routes, gates):
    fronts, tok_rows, width = stream_in.shape
    units = w_gate.shape[2]
    sections = lax.axis_size("layer")
    devices = lax.axis_size("expert")
    flight = devices // GROUP
    half = devices // 2
    tokens = fronts * tok_rows
    few = FEW * flight
    shape = jax.ShapeDtypeStruct
    state = stream_in.reshape(tokens, width)
    routes = jnp.swapaxes(routes[0], 1, 2)
    gates = jnp.swapaxes(gates[0], 1, 2)
    w_gate, w_up, w_down = w_gate[0], w_up[0], w_down[0]
    scale = 1.0 / (fronts * CAP)
    mib = 2**20
    chunks = next(c for c in (7, 8, 4, 2, 1) if width % (c * LANES) == 0)

    def raw_of(count, skip):
        return call(
            functools.partial(rows_body, skip),
            shape((count, width), bf16),
            2,
            traffic=2 * tokens * width,
            limit=8 * mib,
        )(table, state)

    def payload_of(raw, gate_weights, skip):
        count = raw.shape[0]
        return call(
            functools.partial(meta_body, few, skip),
            shape((count, width + LANES), bf16),
            sections + 2,
            limit=8 * mib,
        )(*tables, gate_weights, raw)

    def near_of(payload):
        return [payload] + [passed(payload, "expert", r) for r in range(2, devices, 2)]

    def pairs_of(near, after=()):
        arrived = []
        for part, waits in zip(parts_of(half), ((), after)):
            stacked = call(
                pair_body,
                shape((len(part), *near[0].shape), bf16),
                len(part) + len(waits),
                traffic=2 * half * near[0].size,
                limit=4 * mib + 8 * half * near[0].size,
            )(*[near[q] for q in part], *waits)
            arrived.append(passed(stacked, "expert", 1))
        return arrived

    def held(after, *weights):
        return call(
            held_body,
            tuple(shape(w.shape, bf16) for w in weights),
            1,
            streamed=len(weights),
            scratch=[pltpu.SemaphoreType.DMA((len(weights),))],
            traffic=4 * sum(w.size for w in weights),
            limit=2 * sum(w.size for w in weights) + 2 * mib,
        )(after, *weights)

    def pass_shapes(size, wanted):
        return (
            shape((wanted, width), bf16),
            shape((wanted, width + LANES), bf16),
            shape((1, size), f32),
        )

    def pass_limit(size):
        return 8 * mib + 12 * size * width + 32 * size * size

    def summed(part, chosen):
        bits = [1 << b for b in range(devices.bit_length() - 1)]
        for bit in bits[:-1]:
            part = call(added_body, shape(part.shape, bf16), 2, traffic=6 * part.size)(
                part, passed(part, "expert", bit)
            )
        changed = call(
            changed_body, shape(chosen.shape, bf16), 3, traffic=8 * chosen.size, limit=2 * mib + 32 * chosen.size
        )(part, passed(part, "expert", bits[-1]), chosen)
        return exchanged(changed, "layer")

    def apply_limit(size, wanted):
        return 8 * mib + 16 * sections * wanted * width + 8 * size * width

    def applied(rows, sent, changed):
        size, wanted = rows.shape[0], changed[0].shape[0]
        return call(
            functools.partial(apply_body, sections),
            (shape(rows.shape, bf16), shape((1, 1), f32)),
            2 + sections,
            flops=2 * size * sections * wanted * width,
            traffic=4 * size * width,
            limit=apply_limit(size, wanted),
        )(rows, sent, *changed)

    def passes(rows, wanted, weights):
        size = rows.shape[0]
        count = size // devices
        part, chosen, sent = call(
            functools.partial(pass_body, count, flight),
            pass_shapes(size, wanted),
            5,
            flops=6 * wanted * width * units,
            traffic=2 * size * width,
            limit=pass_limit(size),
        )(rows, gain, *weights)
        return applied(rows, sent, summed(part, chosen))

    def finish(rows, count, weights, sent=None, changed=()):
        size = devices * count
        side = size // 2
        body = functools.partial(final_body, half, flight)
        operands = (rows,)
        more_scratch = []
        if changed:
            body = functools.partial(changed_final_body, half, sections, flight)
            operands = (rows, sent, *changed)
            more_scratch = [pltpu.VMEM(rows.shape, bf16), pltpu.VMEM((1, 1), f32)]
        hidden, raw, near, soon, late = call(
            body,
            (
                shape((size, units), bf16),
                shape((count, width), bf16),
                shape((side, width), bf16),
                shape((side // 2, width + 4 * units), bf16),
                shape((side // 2, width), bf16),
            ),
            5 + (1 + sections if changed else 0),
            scratch=[pltpu.VMEM((devices, -(-count // 8) * 8, units), f32)] + more_scratch,
            flops=6 * size * width * units,
            traffic=6 * width * units,
            limit=8 * mib
            + 24 * min(size, CHUNK) * width
            + 4 * size * width
            + 16 * size * units
            + (apply_limit(size, changed[0].shape[0]) if changed else 0),
        )(*operands, gain, *weights)
        soon = passed(soon, "expert", 1)
        late = passed(late, "expert", 1)
        behind = 2 * devices * units

        def paired(first, far):
            return call(
                functools.partial(paired_body, half, first, half // 2),
                tuple(
                    shape((count, width + (behind if 0 < q < GROUP // 2 else 0)), bf16)
                    for q in range(first, first + half // 2)
                ),
                4,
                traffic=3 * side * width,
                limit=4 * mib + 20 * side * width + 24 * count * behind,
            )(near, far, soon, hidden)

        farther = paired(half // 2, soon)
        arrived = [passed(sums, "expert", 2 * (half // 2 + q)) for q, sums in enumerate(farther)]
        closer = paired(0, late)
        arrived = [passed(closer[q], "expert", 2 * q) for q in range(1, half // 2)] + arrived
        arrived = [closer[0]] + arrived
        select, base = call(
            functools.partial(plan_body, sections, count),
            (shape((tokens, sections * count), bf16), shape((tokens, width), bf16)),
            sections + 2,
            traffic=4 * tokens * width,
            limit=8 * mib,
        )(*tables, state, farther[0])
        fresh = call(
            functools.partial(combine_body, half),
            shape((count, width), bf16),
            half + 2,
            traffic=2 * side * width,
            limit=2 * mib + 16 * count * width + 6 * count * behind,
        )(*arrived, raw, select)
        blocks = exchanged(fresh, "layer")
        gram = call(
            functools.partial(gram_body, scale, width),
            shape((units, GROUP * units), f32),
            2 + GROUP // 2 - 1,
            scratch=[pltpu.VMEM((units, GROUP * units), f32), pltpu.SemaphoreType.DMA(())],
            placed=HBM,
            flops=2 * size * units * units * GROUP,
            traffic=4 * units * units * GROUP,
            limit=8 * mib + 64 * size * units,
        )(hidden, soon, *arrived[1:GROUP // 2])
        new_state = call(
            functools.partial(merge_body, sections),
            shape((tokens, width), bf16),
            sections + 2,
            scratch=[pltpu.VMEM((tokens, width), bf16), pltpu.SemaphoreType.DMA((chunks,))],
            placed=HBM,
            traffic=4 * tokens * width,
            limit=8 * mib + 16 * sections * count * width,
        )(*blocks, select, base)
        return new_state, gram

    def looped(rows, more, weights):
        _, rows = lax.while_loop(
            lambda carry: carry[0][0, 0] > 0.5,
            lambda carry: passes(carry[1], few, weights)[::-1],
            (more, rows),
        )
        return finish(rows, rows.shape[0] // devices, weights)

    table, kept_routes = call(
        functools.partial(table_body, flight), (shape((1, tokens), bf16), shape(routes.shape, routes.dtype)), 1
    )(routes)
    tables = exchanged(table, "layer")
    raw = raw_of(few, 0)
    gate_weights = call(gates_body, shape((flight, tokens), f32), 2)(kept_routes, gates)
    payload = payload_of(raw, gate_weights, 0)
    near = near_of(payload)
    early = held(payload, w_gate)
    pairs = pairs_of(near, early)
    weights = *early, *held(near[1], w_up, w_down)
    size = devices * few
    rows, mode, part, chosen, sent = call(
        functools.partial(first_pass_body, half, sections, few, flight),
        (shape((size, width + LANES), bf16), shape((1, 1), jnp.int32)) + pass_shapes(size, 2 * few),
        half + 6,
        flops=12 * few * width * units,
        traffic=4 * size * width,
        limit=pass_limit(size),
    )(*near, *pairs, gain, *weights)

    def once(share):
        def run(rows, part, chosen, sent, gate_weights, *weights):
            wanted = part.shape[0] // share
            return finish(rows, few, weights, sent, summed(part[:wanted], chosen[:wanted]))

        return run

    def again(share):
        def run(rows, part, chosen, sent, gate_weights, *weights):
            wanted = part.shape[0] // share
            rows, more = applied(rows, sent, summed(part[:wanted], chosen[:wanted]))
            return looped(rows, more, weights)

        return run

    def filled(rows, part, chosen, sent, gate_weights, *weights):
        most = fronts * CAP * flight
        near = near_of(payload_of(raw_of(most - few, few), gate_weights, few))
        rows = call(
            functools.partial(more_stack_body, half),
            shape((devices * most, width + LANES), bf16),
            half + 3,
            traffic=4 * devices * most * width,
            limit=4 * mib + 16 * devices * most * width,
        )(rows, *near, *pairs_of(near))
        rows, more = passes(rows, 4 * few, weights)
        return looped(rows, more, weights)

    shares = (4, 2, 1) if size <= CHUNK else (1, 1, 1)
    branches = [once(share) for share in sorted(set(shares), reverse=True)]
    branches += [again(share) for share in sorted(set(shares[1:]), reverse=True)]
    branches.append(filled)
    mode = mode[0, 0] if size <= CHUNK else jnp.maximum(mode[0, 0] - 1, 0) // 2
    state, gram = lax.switch(
        mode, branches, rows, part, chosen, sent, gate_weights, *weights
    )
    return state.reshape(1, fronts, tok_rows, width), gram[None]


def solution(mesh):
    return jax.shard_map(
        shards,
        mesh=mesh,
        in_specs=(
            P(None, "expert", None),
            P("layer", None),
            P("layer", None, "expert"),
            P("layer", None, "expert"),
            P("layer", "expert", None),
            P("layer", None, "expert", None),
            P("layer", None, "expert", None),
        ),
        out_specs=(P("layer", None, "expert", None), P("layer", "expert", None)),
        check_vma=False,
    )
```

```python
import functools

import jax
import jax.numpy as jnp
from jax import lax
from jax.experimental import pallas as pl
from jax.experimental.pallas import tpu as pltpu
from jax.sharding import PartitionSpec as P

GROUP = 8
CAP = 2
EPSILON = 1e-06
LANES = 128
CHUNK = 128

FEW = 4

STATUS, SOURCE_LAYER, SOURCE_SLOT, WANTED, FULL, DEEP, DEVICE, SLOT, MORE = range(9)
COUNTS = 16
GATES = 32
READY, WAITS = 1.0, 2.0

f32 = jnp.float32
bf16 = jnp.bfloat16
VMEM = pl.BlockSpec(memory_space=pltpu.VMEM)
HBM = pl.BlockSpec(memory_space=pltpu.HBM)


def whereabouts():
    return lax.axis_index("layer").astype(jnp.int32), lax.axis_index("expert").astype(jnp.int32)


def call(
    body, out_shape, n_in, scratch=(), flops=0, traffic=0, limit=2 * 2**20, streamed=0, placed=None
):
    return pl.pallas_call(
        body,
        out_shape=out_shape,
        in_specs=[VMEM] * n_in + [HBM] * streamed,
        out_specs=placed or jax.tree.map(lambda s: VMEM, out_shape),
        scratch_shapes=list(scratch),
        compiler_params=pltpu.CompilerParams(vmem_limit_bytes=limit),
        cost_estimate=pl.CostEstimate(flops=flops, bytes_accessed=traffic, transcendentals=0),
    )


def iota(shape, dim):
    return lax.broadcasted_iota(jnp.int32, shape, dim)


def stack_rows(rows):
    return jnp.concatenate(rows, axis=0)


def lane_of(extra, number):
    return extra[:, number:number + 1]


def across(column):
    size = column.shape[0]
    same = iota((size, size), 0) == iota((size, size), 1)
    return jnp.sum(jnp.where(same, column, 0.0), axis=0, keepdims=True)


def ranked(rows):
    size = rows[0].shape[1]
    upto = (iota((size, size), 0) <= iota((size, size), 1)).astype(f32).astype(bf16)
    rank = jnp.dot(stack_rows(rows).astype(bf16), upto, preferred_element_type=f32)
    return [rank[r:r + 1] * row for r, row in enumerate(rows)]


def selection(rank, count):
    wanted = (iota((count, rank.shape[1]), 0) + 1).astype(f32)
    return jnp.where(rank == wanted, 1.0, 0.0)


def normalized(rows, gain):
    scale = lax.rsqrt(jnp.mean(rows * rows, axis=-1, keepdims=True) + EPSILON)
    return (rows * scale * gain).astype(bf16)


def by_front(routes_ref, of_front):
    return jnp.concatenate([of_front(f) for f in range(routes_ref.shape[0])], axis=1)


def table_body(flight, routes_ref, table_ref, kept_ref):
    kept_ref[...] = routes_ref[...]
    table_ref[...] = by_front(
        routes_ref,
        lambda f: jnp.max(jnp.where(routes_ref[f] < flight, 1.0, 0.0), axis=0, keepdims=True),
    ).astype(bf16)


def held_body(after_ref, *refs):
    count = len(refs) // 2
    sems = refs[-1]
    copies = [pltpu.make_async_copy(refs[i], refs[count + i], sems.at[i]) for i in range(count)]
    for copy in copies:
        copy.start()
    for copy in copies:
        copy.wait()


def rows_body(skip, table_ref, state_ref, raw_ref):
    select = selection(ranked([table_ref[...].astype(f32)])[0] - skip, raw_ref.shape[0])
    raw_ref[...] = jnp.dot(select.astype(bf16), state_ref[...], preferred_element_type=f32).astype(bf16)


def gates_body(routes_ref, gates_ref, weights_ref):
    weights_ref[...] = stack_rows([
        by_front(
            routes_ref,
            lambda f: jnp.sum(jnp.where(routes_ref[f] == expert, gates_ref[f], 0.0), axis=0, keepdims=True),
        )
        for expert in range(weights_ref.shape[0])
    ])


def before(layer, a, b):
    return jnp.where((layer ^ a) < (layer ^ b), 1.0, 0.0)


def between(layer, a, b, routed):
    total = jnp.zeros_like(routed[0])
    for r, row in enumerate(routed):
        if r not in (a, b):
            total = jnp.maximum(total, row * before(layer, a, r) * before(layer, r, b))
    return total


def number_of(layer, r, sections):
    return sum(jnp.where((layer ^ r) == other, float(other), 0.0) for other in range(sections))


def meta_body(few, skip, *refs):
    tables, (gates_ref, raw_ref, payload_ref) = refs[:-3], refs[-3:]
    layer, member = whereabouts()
    count, width = raw_ref.shape
    routed = [ref[...].astype(f32) for ref in tables]
    ranks = ranked(routed)
    waits = source_layer = source_slot = wanted = jnp.zeros_like(routed[0])
    for r in range(1, len(routed)):
        source = routed[r] * before(layer, r, 0) * (1.0 - between(layer, r, 0, routed))
        waits = waits + source
        source_layer = source_layer + source * number_of(layer, r, len(routed))
        source_slot = source_slot + source * ranks[r]
        wanted = jnp.maximum(wanted, routed[r] * before(layer, 0, r))
    status = jnp.where(waits > 0.5, WAITS, READY)
    full = sum(jnp.where(rank > few, 1.0, 0.0) for rank in ranks)
    deep = jnp.where(sum(routed) > 2.5, 1.0, 0.0)
    counts = [jnp.zeros_like(deep) for _ in routed]
    for r, row in enumerate(routed):
        later = jnp.zeros_like(row)
        for other, other_row in enumerate(routed):
            if other != r:
                later = jnp.maximum(later, other_row * before(layer, r, other))
        for place in range(len(counts)):
            counts[place] = counts[place] + row * later * jnp.where((layer ^ r) == place, 1.0, 0.0)
    gates = gates_ref[...]
    high = gates.astype(bf16).astype(f32)
    named = {STATUS: status, SOURCE_LAYER: source_layer, SOURCE_SLOT: source_slot, WANTED: wanted}
    named.update({FULL: full, DEEP: deep})
    named.update({COUNTS + place: row for place, row in enumerate(counts)})
    for expert in range(gates.shape[0]):
        named[GATES + expert] = high[expert:expert + 1]
        named[GATES + gates.shape[0] + expert] = (gates - high)[expert:expert + 1]
    last = -(-(max(named) + 1) // 8) * 8
    empty = jnp.zeros_like(deep)
    table = [named.get(number, empty) for number in range(last)]
    table = stack_rows(table + [jnp.zeros((LANES - last, deep.shape[1]), f32)]).astype(bf16)
    select = selection(ranks[0] - skip, count)
    left = stack_rows([select, jnp.ones_like(select)]).astype(bf16)
    both = lax.dot_general(left, table, (((1,), (1,)), ((), ())), preferred_element_type=f32)
    lane = iota((count, LANES), 1)
    by_column = jnp.logical_or(lane == FULL, lane == DEEP)
    by_column = jnp.logical_or(by_column, jnp.logical_and(lane >= COUNTS, lane < GATES))
    extra = jnp.where(by_column, both[count:], both[:count])
    extra = jnp.where(lane == DEVICE, jnp.full((count, LANES), member + 1, jnp.int32).astype(f32), extra)
    extra = jnp.where(lane == SLOT, (iota((count, LANES), 0) + (1 + skip)).astype(f32), extra)
    payload_ref[:, :width] = raw_ref[...]
    payload_ref[:, width:] = extra.astype(bf16)


def distances(half):
    return [2 * q for q in range(half)] + [2 * q + 1 for q in range(half)]


def stack_body(half, *refs):
    near, pair_ref, rows_ref = refs[:half], refs[half], refs[half + 1]
    blocks = [ref[...] for ref in near] + [pair_ref[q] for q in range(half)]
    count = blocks[0].shape[0]
    if count % 16 == 0:
        for place, block in enumerate(blocks):
            rows_ref[place * count:(place + 1) * count] = block
    else:
        rows_ref[...] = stack_rows([block.astype(f32) for block in blocks]).astype(bf16)


def pair_body(*refs):
    out_ref = refs[-1]
    for q in range(out_ref.shape[0]):
        out_ref[q] = refs[q][...]


def more_stack_body(half, rows_ref, *refs):
    near, pair_ref, into_ref = refs[:half], refs[half], refs[half + 1]
    more = [ref[...] for ref in near] + [pair_ref[q] for q in range(half)]
    count = more[0].shape[0]
    if count % 16 == 0:
        for place, block in enumerate(more):
            into_ref[2 * place * count:(2 * place + 1) * count] = rows_ref[place * count:(place + 1) * count]
            into_ref[(2 * place + 1) * count:(2 * place + 2) * count] = block
        return
    rows = rows_ref[...].astype(f32)
    stacked = []
    for place, block in enumerate(more):
        stacked += [rows[place * count:(place + 1) * count], block.astype(f32)]
    into_ref[...] = stack_rows(stacked).astype(bf16)


def first_pass_body(half, sections, count, flight, *refs):
    gathered, refs = refs[:half + 1], refs[half + 1:]
    gain_ref, gate_ref, up_ref, down_ref, rows_ref, mode_ref, part_ref, chosen_ref, sent_ref = refs
    stack_body(half, *gathered, rows_ref)
    pass_body(count, flight, rows_ref, gain_ref, gate_ref, up_ref, down_ref, part_ref, chosen_ref, sent_ref)
    extra = rows_ref[:, gain_ref.shape[1]:].astype(f32)
    most = jnp.max(extra, axis=0, keepdims=True)
    total = jnp.sum(jnp.where(lane_of(extra, SLOT) == 1.0, extra, 0.0), axis=0, keepdims=True)
    total = jnp.max(total[:, COUNTS:COUNTS + sections], axis=1, keepdims=True)
    wanted_count = part_ref.shape[0]
    mode = jnp.where(total > wanted_count // 4, 1, 0) + jnp.where(total > wanted_count // 2, 1, 0)
    again = jnp.where(total > wanted_count // 2, 4, 3)
    again = jnp.where(total > wanted_count, again, jnp.where(lane_of(most, DEEP) > 0.5, again, mode))
    mode_ref[...] = jnp.where(lane_of(most, FULL) > 0.5, 5, again)


def activated(rows, gate_ref, up_ref):
    gate = jnp.dot(rows, gate_ref[...], preferred_element_type=f32)
    up = jnp.dot(rows, up_ref[...], preferred_element_type=f32)
    return gate / (1.0 + jnp.exp(-gate)) * up


def weight_of(extra, member, flight):
    lane = iota(extra.shape, 1)
    expert = member // GROUP
    mine = jnp.logical_or(lane == GATES + expert, lane == GATES + flight + expert)
    return jnp.sum(jnp.where(mine, extra, 0.0), axis=1, keepdims=True)


def pass_body(count, flight, rows_ref, gain_ref, gate_ref, up_ref, down_ref, part_ref, chosen_ref, sent_ref):
    member = whereabouts()[1]
    width = gain_ref.shape[1]
    wanted_count = part_ref.shape[0]
    extra = rows_ref[:, width:].astype(f32)
    wanted = lane_of(extra, WANTED)
    eligible = jnp.where(lane_of(extra, STATUS) == READY, wanted, 0.0)
    number = lane_of(extra, DEVICE) * count + lane_of(extra, SLOT)
    upto = number <= across(number)
    rank = jnp.sum(jnp.where(upto, eligible, 0.0), axis=0, keepdims=True) * across(eligible)
    select = selection(rank, wanted_count)
    chosen = jnp.dot(select.astype(bf16), rows_ref[...], preferred_element_type=f32)
    taken = jnp.sum(select, axis=0, keepdims=True)
    more = jnp.max(across(wanted) - taken, axis=1, keepdims=True)
    sent_ref[...] = taken
    lanes = chosen[:, width:]
    lane = iota(lanes.shape, 1)
    chosen_ref[:, :width] = chosen[:, :width].astype(bf16)
    chosen_ref[:, width:] = jnp.where(lane == MORE, more, lanes).astype(bf16)
    weight = weight_of(lanes, member, flight)
    hidden = activated(normalized(chosen[:, :width], gain_ref[...]), gate_ref, up_ref)
    if flight > 1:
        hidden = jnp.where(weight > 0.0, hidden, 0.0)
    share = jnp.dot(hidden.astype(bf16), down_ref[...], preferred_element_type=f32) * weight
    part_ref[...] = share.astype(bf16)


def added_body(a_ref, b_ref, out_ref):
    out_ref[...] = (a_ref[...].astype(f32) + b_ref[...].astype(f32)).astype(bf16)


def changed_body(a_ref, b_ref, chosen_ref, out_ref):
    width = a_ref.shape[1]
    total = chosen_ref[:, :width].astype(f32) + a_ref[...].astype(f32) + b_ref[...].astype(f32)
    out_ref[:, :width] = total.astype(bf16)
    out_ref[:, width:] = chosen_ref[:, width:]


def by_chunks(size, run):
    if size <= CHUNK:
        run(slice(0, size))
        return

    @pl.loop(0, size // CHUNK)
    def _(i):
        run(pl.ds(pl.multiple_of(i * CHUNK, CHUNK), CHUNK))


def apply_body(sections, rows_ref, sent_ref, *refs):
    changed, into_ref, more_ref = refs[:sections], refs[sections], refs[sections + 1]
    layer = whereabouts()[0]
    width = rows_ref.shape[1] - LANES
    names = [ref[:, width:].astype(f32) for ref in changed]
    fresh = stack_rows([ref[:, :width].astype(f32) for ref in changed[1:]]).astype(bf16)
    columns = [(across(lane_of(name, DEVICE)), across(lane_of(name, SLOT))) for name in names]
    more = names[0]
    for name in names[1:]:
        more = jnp.maximum(more, name)
    more_ref[...] = jnp.max(lane_of(more, MORE), axis=0, keepdims=True)
    size = rows_ref.shape[0]
    taken = sent_ref[...]

    def run(part):
        extra = rows_ref[part, width:].astype(f32)
        waits = jnp.where(lane_of(extra, STATUS) == WAITS, 1.0, 0.0)
        matches = []
        for r in range(1, sections):
            device, slot = columns[r]
            match = jnp.where(lane_of(extra, DEVICE) == device, waits, 0.0)
            match = match * jnp.where(lane_of(extra, SOURCE_SLOT) == slot, 1.0, 0.0)
            from_it = jnp.where(lane_of(extra, SOURCE_LAYER) == number_of(layer, r, sections), 1.0, 0.0)
            matches.append(match * from_it)
        match = jnp.concatenate(matches, axis=1)
        arrived = jnp.max(match, axis=1, keepdims=True)
        new = jnp.dot(match.astype(bf16), fresh, preferred_element_type=f32)
        old = rows_ref[part, :width].astype(f32)
        into_ref[part, :width] = jnp.where(arrived > 0.5, new, old).astype(bf16)
        lane = iota(extra.shape, 1)
        extra = jnp.where(jnp.logical_and(lane == STATUS, arrived > 0.5), READY, extra)
        if size <= CHUNK:
            own = iota((size, size), 0) == iota((size, size), 1)
            gone = jnp.sum(jnp.where(own, taken, 0.0), axis=1, keepdims=True)
        else:
            first = part.start
            row = iota((CHUNK, size), 0) + first == iota((CHUNK, size), 1)
            gone = jnp.sum(jnp.where(row, taken, 0.0), axis=1, keepdims=True)
        extra = jnp.where(jnp.logical_and(lane == WANTED, gone > 0.5), 0.0, extra)
        into_ref[part, width:] = extra.astype(bf16)

    by_chunks(size, run)


def changed_final_body(half, sections, flight, rows_ref, sent_ref, *refs):
    changed, rest, scratch = refs[:sections], refs[sections:-2], refs[-2:]
    into_ref, more_ref = scratch
    apply_body(sections, rows_ref, sent_ref, *changed, into_ref, more_ref)
    final_body(half, flight, into_ref, *rest)


def final_body(
    half, flight, rows_ref, gain_ref, gate_ref, up_ref, down_ref,
    hidden_ref, raw_ref, near_ref, soon_ref, late_ref, ordered_ref
):
    member = whereabouts()[1]
    width = gain_ref.shape[1]
    units = hidden_ref.shape[1]
    size = rows_ref.shape[0]
    side = size // 2
    count = raw_ref.shape[0]
    raw_ref[...] = rows_ref[:, :width].astype(f32)[:count].astype(bf16) if size <= CHUNK else rows_ref[:count, :width]
    hidden_rows = []

    def run(part, of_part=None):
        extra = rows_ref[part, width:].astype(f32)
        weight = weight_of(extra, member, flight)
        hidden = activated(normalized(rows_ref[part, :width].astype(f32), gain_ref[...]), gate_ref, up_ref)
        if flight > 1:
            hidden = jnp.where(weight > 0.0, hidden, 0.0)
        share = jnp.dot(hidden.astype(bf16), down_ref[...], preferred_element_type=f32) * weight
        return hidden, share

    if size <= CHUNK:
        hidden, share = run(slice(0, size))
        near_ref[...] = share[:side].astype(bf16)
        late_ref[...] = share[side:side + side // 2].astype(bf16)
        soon_ref[:, :width] = share[side + side // 2:].astype(bf16)
        for place, r in enumerate(distances(half)):
            ordered_ref[member ^ r, :count] = hidden[place * count:(place + 1) * count]
    else:
        blocks = CHUNK // count

        def part_run(first, size, into_ref, block, odd):
            @pl.loop(0, size // CHUNK)
            def _(i):
                at = pl.multiple_of(i * CHUNK, CHUNK)
                hidden, share = run(pl.ds(pl.multiple_of(first + at, CHUNK), CHUNK))
                into_ref[pl.ds(at, CHUNK), :width] = share.astype(bf16)
                for b in range(blocks):
                    distance = 2 * (block + i * blocks + b) + odd
                    ordered_ref[member ^ distance] = hidden[b * count:(b + 1) * count]

        part_run(0, side, near_ref, 0, 0)
        part_run(side, side // 2, late_ref, 0, 1)
        part_run(side + side // 2, side // 2, soon_ref, half // 2, 1)
    ordered_rows = stack_rows([ordered_ref[source, :count] for source in range(2 * half)])
    hidden_rows = ordered_rows.astype(bf16)
    hidden_ref[...] = hidden_rows
    quarter = side // 2
    for i in range(4):
        rows_of = slice(i * quarter, (i + 1) * quarter)
        values = ordered_rows[rows_of].astype(bf16) if quarter % 16 else hidden_rows[rows_of]
        soon_ref[:, width + i * units:width + (i + 1) * units] = values


def regrouped(rows, count):
    return jnp.concatenate([rows[i:i + count] for i in range(0, rows.shape[0], count)], axis=1)


def spread(block, units):
    return stack_rows([block[:, i:i + units] for i in range(0, block.shape[1], units)])


def their_hidden(soon_ref, width, units):
    behind = soon_ref[:, width:].astype(f32)
    return stack_rows([behind[:, i:i + units] for i in range(0, behind.shape[1], units)])


def paired_body(half, first, number, near_ref, far_ref, soon_ref, hidden_ref, *out_refs):
    width = near_ref.shape[1]
    units = hidden_ref.shape[1]
    count = near_ref.shape[0] // half
    mine = near_ref[...].astype(f32)[first * count:(first + number) * count]
    total = mine + far_ref[:, :width].astype(f32)
    both = None
    for q, ref in enumerate(out_refs):
        ref[:, :width] = total[q * count:(q + 1) * count].astype(bf16)
        if ref.shape[1] > width:
            if both is None:
                both = [hidden_ref[...].astype(f32), their_hidden(soon_ref, width, units)]
                both = jnp.concatenate([regrouped(rows, count) for rows in both], axis=1).astype(bf16)
            ref[:, width:] = both


def combine_body(half, *refs):
    shares, raw_ref, out_ref = refs[:half], refs[half], refs[-1]
    width = raw_ref.shape[1]
    update = shares[0][:, :width].astype(f32)
    for ref in shares[1:]:
        update = update + ref[:, :width].astype(f32)
    out_ref[...] = (raw_ref[...].astype(f32) + update).astype(bf16)


def plan_body(sections, count, *refs):
    tables = refs[:sections]
    state_ref, _, select_ref, base_ref = refs[sections:]
    layer = whereabouts()[0]
    routed = [ref[...].astype(f32) for ref in tables]
    shown = [row * jnp.where((layer ^ r) <= layer, 1.0, 0.0) for r, row in enumerate(routed)]
    select = []
    for r, rank in enumerate(ranked(routed)):
        later = jnp.zeros_like(rank)
        for other, row in enumerate(shown):
            if other != r:
                later = jnp.maximum(later, row * before(layer, r, other))
        select.append(selection(jnp.where(shown[r] > 0.5, rank * (1.0 - later), 0.0), count))
    select = stack_rows(select).astype(bf16)
    size = select.shape[0]
    same = (iota((size, size), 0) == iota((size, size), 1)).astype(f32).astype(bf16)
    over = (((0,), (0,)), ((), ()))
    turned = lax.dot_general(select, same, over, preferred_element_type=f32)
    select_ref[...] = turned.astype(bf16)
    hit = jnp.sum(turned, axis=1, keepdims=True)
    base_ref[...] = jnp.where(hit > 0.5, 0.0, state_ref[...].astype(f32)).astype(bf16)


def merge_body(sections, *refs):
    blocks = refs[:sections]
    select_ref, base_ref, into_ref, held_ref, sems = refs[sections:]
    width = base_ref.shape[1]
    rows = stack_rows([block[...].astype(f32) for block in blocks]).astype(bf16)
    copies = []
    chunks = sems.shape[0]
    step = width // chunks
    for i in range(chunks):
        part = slice(i * step, (i + 1) * step)
        fresh = jnp.dot(select_ref[...], rows[:, part], preferred_element_type=f32)
        held_ref[:, part] = (fresh + base_ref[:, part].astype(f32)).astype(bf16)
        copies.append(pltpu.make_async_copy(held_ref.at[:, part], into_ref.at[:, part], sems.at[i]))
        copies[-1].start()
    for copy in copies:
        copy.wait()


def gram_body(scale, width, mine_ref, far_ref, *refs):
    others, (out_ref, held_ref, sem) = refs[:-3], refs[-3:]
    member = whereabouts()[1] % GROUP
    mine = mine_ref[...]
    size, units = mine.shape
    blocks = [mine, their_hidden(far_ref, width, units).astype(bf16)]
    for ref in others:
        both = spread(ref[:, width:].astype(f32), units).astype(bf16)
        blocks += [both[:size], both[size:]]
    for r, block in enumerate(blocks):
        term = scale * lax.dot_general(
            mine, block, (((0,), (0,)), ((), ())), preferred_element_type=f32
        )
        held_ref[:, pl.ds(pl.multiple_of((member ^ r) * units, units), units)] = term
    copy = pltpu.make_async_copy(held_ref, out_ref, sem)
    copy.start()
    copy.wait()


def passed(value, axis, r):
    return lax.ppermute(value, axis, [(i, i ^ r) for i in range(lax.axis_size(axis))])


def exchanged(value, axis):
    return [value] + [passed(value, axis, r) for r in range(1, lax.axis_size(axis))]


def shards(stream_in, gain, w_gate, w_up, w_down, routes, gates):
    fronts, tok_rows, width = stream_in.shape
    units = w_gate.shape[2]
    sections = lax.axis_size("layer")
    devices = lax.axis_size("expert")
    flight = devices // GROUP
    half = devices // 2
    tokens = fronts * tok_rows
    few = FEW * flight
    shape = jax.ShapeDtypeStruct
    state = stream_in.reshape(tokens, width)
    routes = jnp.swapaxes(routes[0], 1, 2)
    gates = jnp.swapaxes(gates[0], 1, 2)
    w_gate, w_up, w_down = w_gate[0], w_up[0], w_down[0]
    scale = 1.0 / (fronts * CAP)
    mib = 2**20
    chunks = next(c for c in (7, 8, 4, 2, 1) if width % (c * LANES) == 0)

    def raw_of(count, skip):
        return call(
            functools.partial(rows_body, skip),
            shape((count, width), bf16),
            2,
            traffic=2 * tokens * width,
            limit=8 * mib,
        )(table, state)

    def payload_of(raw, gate_weights, skip):
        count = raw.shape[0]
        return call(
            functools.partial(meta_body, few, skip),
            shape((count, width + LANES), bf16),
            sections + 2,
            limit=8 * mib,
        )(*tables, gate_weights, raw)

    def near_of(payload):
        return [payload] + [passed(payload, "expert", r) for r in range(2, devices, 2)]

    def pair_of(near, after=()):
        stacked = call(
            pair_body,
            shape((half, *near[0].shape), bf16),
            half + len(after),
            traffic=4 * half * near[0].size,
            limit=4 * mib + 16 * half * near[0].size,
        )(*near, *after)
        return passed(stacked, "expert", 1)

    def held(after, *weights):
        return call(
            held_body,
            tuple(shape(w.shape, bf16) for w in weights),
            1,
            streamed=len(weights),
            scratch=[pltpu.SemaphoreType.DMA((len(weights),))],
            traffic=4 * sum(w.size for w in weights),
            limit=2 * sum(w.size for w in weights) + 2 * mib,
        )(after, *weights)

    def pass_shapes(size, wanted):
        return (
            shape((wanted, width), bf16),
            shape((wanted, width + LANES), bf16),
            shape((1, size), f32),
        )

    def pass_limit(size):
        return 8 * mib + 12 * size * width + 32 * size * size

    def summed(part, chosen):
        bits = [1 << b for b in range(devices.bit_length() - 1)]
        for bit in bits[:-1]:
            part = call(added_body, shape(part.shape, bf16), 2, traffic=6 * part.size)(
                part, passed(part, "expert", bit)
            )
        changed = call(
            changed_body, shape(chosen.shape, bf16), 3, traffic=8 * chosen.size, limit=2 * mib + 32 * chosen.size
        )(part, passed(part, "expert", bits[-1]), chosen)
        return exchanged(changed, "layer")

    def apply_limit(size, wanted):
        return 8 * mib + 16 * sections * wanted * width + 8 * size * width

    def applied(rows, sent, changed):
        size, wanted = rows.shape[0], changed[0].shape[0]
        return call(
            functools.partial(apply_body, sections),
            (shape(rows.shape, bf16), shape((1, 1), f32)),
            2 + sections,
            flops=2 * size * sections * wanted * width,
            traffic=4 * size * width,
            limit=apply_limit(size, wanted),
        )(rows, sent, *changed)

    def passes(rows, wanted, weights):
        size = rows.shape[0]
        count = size // devices
        part, chosen, sent = call(
            functools.partial(pass_body, count, flight),
            pass_shapes(size, wanted),
            5,
            flops=6 * wanted * width * units,
            traffic=2 * size * width,
            limit=pass_limit(size),
        )(rows, gain, *weights)
        return applied(rows, sent, summed(part, chosen))

    def finish(rows, count, weights, sent=None, changed=()):
        size = devices * count
        side = size // 2
        body = functools.partial(final_body, half, flight)
        operands = (rows,)
        more_scratch = []
        if changed:
            body = functools.partial(changed_final_body, half, sections, flight)
            operands = (rows, sent, *changed)
            more_scratch = [pltpu.VMEM(rows.shape, bf16), pltpu.VMEM((1, 1), f32)]
        hidden, raw, near, soon, late = call(
            body,
            (
                shape((size, units), bf16),
                shape((count, width), bf16),
                shape((side, width), bf16),
                shape((side // 2, width + 4 * units), bf16),
                shape((side // 2, width), bf16),
            ),
            5 + (1 + sections if changed else 0),
            scratch=[pltpu.VMEM((devices, -(-count // 8) * 8, units), f32)] + more_scratch,
            flops=6 * size * width * units,
            traffic=6 * width * units,
            limit=8 * mib
            + 24 * min(size, CHUNK) * width
            + 4 * size * width
            + 16 * size * units
            + (apply_limit(size, changed[0].shape[0]) if changed else 0),
        )(*operands, gain, *weights)
        soon = passed(soon, "expert", 1)
        late = passed(late, "expert", 1)
        behind = 2 * devices * units

        def paired(first, far):
            return call(
                functools.partial(paired_body, half, first, half // 2),
                tuple(
                    shape((count, width + (behind if 0 < q < GROUP // 2 else 0)), bf16)
                    for q in range(first, first + half // 2)
                ),
                4,
                traffic=3 * side * width,
                limit=4 * mib + 20 * side * width + 24 * count * behind,
            )(near, far, soon, hidden)

        farther = paired(half // 2, soon)
        arrived = [passed(sums, "expert", 2 * (half // 2 + q)) for q, sums in enumerate(farther)]
        closer = paired(0, late)
        arrived = [passed(closer[q], "expert", 2 * q) for q in range(1, half // 2)] + arrived
        arrived = [closer[0]] + arrived
        select, base = call(
            functools.partial(plan_body, sections, count),
            (shape((tokens, sections * count), bf16), shape((tokens, width), bf16)),
            sections + 2,
            traffic=4 * tokens * width,
            limit=8 * mib,
        )(*tables, state, farther[0])
        fresh = call(
            functools.partial(combine_body, half),
            shape((count, width), bf16),
            half + 2,
            traffic=2 * side * width,
            limit=2 * mib + 16 * count * width + 6 * count * behind,
        )(*arrived, raw, select)
        blocks = exchanged(fresh, "layer")
        gram = call(
            functools.partial(gram_body, scale, width),
            shape((units, GROUP * units), f32),
            2 + GROUP // 2 - 1,
            scratch=[pltpu.VMEM((units, GROUP * units), f32), pltpu.SemaphoreType.DMA(())],
            placed=HBM,
            flops=2 * size * units * units * GROUP,
            traffic=4 * units * units * GROUP,
            limit=8 * mib + 64 * size * units,
        )(hidden, soon, *arrived[1:GROUP // 2])
        new_state = call(
            functools.partial(merge_body, sections),
            shape((tokens, width), bf16),
            sections + 2,
            scratch=[pltpu.VMEM((tokens, width), bf16), pltpu.SemaphoreType.DMA((chunks,))],
            placed=HBM,
            traffic=4 * tokens * width,
            limit=8 * mib + 16 * sections * count * width,
        )(*blocks, select, base)
        return new_state, gram

    def looped(rows, more, wanted, weights):
        _, rows = lax.while_loop(
            lambda carry: carry[0][0, 0] > 0.5,
            lambda carry: passes(carry[1], wanted, weights)[::-1],
            (more, rows),
        )
        return finish(rows, rows.shape[0] // devices, weights)

    table, kept_routes = call(
        functools.partial(table_body, flight), (shape((1, tokens), bf16), shape(routes.shape, routes.dtype)), 1
    )(routes)
    tables = exchanged(table, "layer")
    raw = raw_of(few, 0)
    gate_weights = call(gates_body, shape((flight, tokens), f32), 2)(kept_routes, gates)
    payload = payload_of(raw, gate_weights, 0)
    near = near_of(payload)
    early = held(payload, w_gate)
    pair = pair_of(near, early)
    weights = *early, *held(near[1], w_up, w_down)
    size = devices * few
    rows, mode, part, chosen, sent = call(
        functools.partial(first_pass_body, half, sections, few, flight),
        (shape((size, width + LANES), bf16), shape((1, 1), jnp.int32)) + pass_shapes(size, 2 * few),
        half + 5,
        flops=12 * few * width * units,
        traffic=4 * size * width,
        limit=pass_limit(size),
    )(*near, pair, gain, *weights)

    def once(share):
        def run(rows, part, chosen, sent, gate_weights, *weights):
            wanted = part.shape[0] // share
            return finish(rows, few, weights, sent, summed(part[:wanted], chosen[:wanted]))

        return run

    def again(share):
        def run(rows, part, chosen, sent, gate_weights, *weights):
            wanted = part.shape[0] // share
            rows, more = applied(rows, sent, summed(part[:wanted], chosen[:wanted]))
            return looped(rows, more, few // 2, weights)

        return run

    def filled(rows, part, chosen, sent, gate_weights, *weights):
        most = fronts * CAP * flight
        near = near_of(payload_of(raw_of(most - few, few), gate_weights, few))
        rows = call(
            functools.partial(more_stack_body, half),
            shape((devices * most, width + LANES), bf16),
            half + 2,
            traffic=4 * devices * most * width,
            limit=4 * mib + 16 * devices * most * width,
        )(rows, *near, pair_of(near))
        rows, more = passes(rows, 2 * few, weights)
        return looped(rows, more, 2 * few, weights)

    shares = (4, 2, 1) if size <= CHUNK else (1, 1, 1)
    branches = [once(share) for share in sorted(set(shares), reverse=True)]
    branches += [again(share) for share in sorted(set(shares[1:]), reverse=True)]
    branches.append(filled)
    mode = mode[0, 0] if size <= CHUNK else jnp.maximum(mode[0, 0] - 1, 0) // 2
    state, gram = lax.switch(
        mode, branches, rows, part, chosen, sent, gate_weights, *weights
    )
    return state.reshape(1, fronts, tok_rows, width), gram[None]


def solution(mesh):
    return jax.shard_map(
        shards,
        mesh=mesh,
        in_specs=(
            P(None, "expert", None),
            P("layer", None),
            P("layer", None, "expert"),
            P("layer", None, "expert"),
            P("layer", "expert", None),
            P("layer", None, "expert", None),
            P("layer", None, "expert", None),
        ),
        out_specs=(P("layer", None, "expert", None), P("layer", "expert", None)),
        check_vma=False,
    )
```

```python
import functools

import jax
import jax.numpy as jnp
from jax import lax
from jax.experimental import pallas as pl
from jax.experimental.pallas import tpu as pltpu
from jax.sharding import PartitionSpec as P

GROUP = 8
CAP = 2
EPSILON = 1e-06
LANES = 128
CHUNK = 128

FEW = 4

STATUS, SOURCE_LAYER, SOURCE_SLOT, WANTED, FULL, DEEP, DEVICE, SLOT, MORE = range(9)
COUNTS = 16
GATES = 32
READY, WAITS = 1.0, 2.0

f32 = jnp.float32
bf16 = jnp.bfloat16
VMEM = pl.BlockSpec(memory_space=pltpu.VMEM)
HBM = pl.BlockSpec(memory_space=pltpu.HBM)


def whereabouts():
    return lax.axis_index("layer").astype(jnp.int32), lax.axis_index("expert").astype(jnp.int32)


def call(
    body, out_shape, n_in, scratch=(), flops=0, traffic=0, limit=2 * 2**20, streamed=0, placed=None
):
    return pl.pallas_call(
        body,
        out_shape=out_shape,
        in_specs=[VMEM] * n_in + [HBM] * streamed,
        out_specs=placed or jax.tree.map(lambda s: VMEM, out_shape),
        scratch_shapes=list(scratch),
        compiler_params=pltpu.CompilerParams(vmem_limit_bytes=limit),
        cost_estimate=pl.CostEstimate(flops=flops, bytes_accessed=traffic, transcendentals=0),
    )


def iota(shape, dim):
    return lax.broadcasted_iota(jnp.int32, shape, dim)


def stack_rows(rows):
    return jnp.concatenate(rows, axis=0)


def lane_of(extra, number):
    return extra[:, number:number + 1]


def across(column):
    size = column.shape[0]
    same = iota((size, size), 0) == iota((size, size), 1)
    return jnp.sum(jnp.where(same, column, 0.0), axis=0, keepdims=True)


def ranked(rows):
    size = rows[0].shape[1]
    upto = (iota((size, size), 0) <= iota((size, size), 1)).astype(f32).astype(bf16)
    rank = jnp.dot(stack_rows(rows).astype(bf16), upto, preferred_element_type=f32)
    return [rank[r:r + 1] * row for r, row in enumerate(rows)]


def selection(rank, count):
    wanted = (iota((count, rank.shape[1]), 0) + 1).astype(f32)
    return jnp.where(rank == wanted, 1.0, 0.0)


def normalized(rows, gain):
    scale = lax.rsqrt(jnp.mean(rows * rows, axis=-1, keepdims=True) + EPSILON)
    return (rows * scale * gain).astype(bf16)


def by_front(routes_ref, of_front):
    return jnp.concatenate([of_front(f) for f in range(routes_ref.shape[0])], axis=1)


def table_body(flight, routes_ref, table_ref, kept_ref):
    kept_ref[...] = routes_ref[...]
    table_ref[...] = by_front(
        routes_ref,
        lambda f: jnp.max(jnp.where(routes_ref[f] < flight, 1.0, 0.0), axis=0, keepdims=True),
    ).astype(bf16)


def held_body(after_ref, *refs):
    count = len(refs) // 2
    sems = refs[-1]
    copies = [pltpu.make_async_copy(refs[i], refs[count + i], sems.at[i]) for i in range(count)]
    for copy in copies:
        copy.start()
    for copy in copies:
        copy.wait()


def rows_body(skip, table_ref, state_ref, raw_ref):
    select = selection(ranked([table_ref[...].astype(f32)])[0] - skip, raw_ref.shape[0])
    raw_ref[...] = jnp.dot(select.astype(bf16), state_ref[...], preferred_element_type=f32).astype(bf16)


def gates_body(routes_ref, gates_ref, weights_ref):
    weights_ref[...] = stack_rows([
        by_front(
            routes_ref,
            lambda f: jnp.sum(jnp.where(routes_ref[f] == expert, gates_ref[f], 0.0), axis=0, keepdims=True),
        )
        for expert in range(weights_ref.shape[0])
    ])


def before(layer, a, b):
    return jnp.where((layer ^ a) < (layer ^ b), 1.0, 0.0)


def between(layer, a, b, routed):
    total = jnp.zeros_like(routed[0])
    for r, row in enumerate(routed):
        if r not in (a, b):
            total = jnp.maximum(total, row * before(layer, a, r) * before(layer, r, b))
    return total


def number_of(layer, r, sections):
    return sum(jnp.where((layer ^ r) == other, float(other), 0.0) for other in range(sections))


def meta_body(few, skip, *refs):
    tables, (gates_ref, raw_ref, payload_ref) = refs[:-3], refs[-3:]
    layer, member = whereabouts()
    count, width = raw_ref.shape
    routed = [ref[...].astype(f32) for ref in tables]
    ranks = ranked(routed)
    waits = source_layer = source_slot = wanted = jnp.zeros_like(routed[0])
    for r in range(1, len(routed)):
        source = routed[r] * before(layer, r, 0) * (1.0 - between(layer, r, 0, routed))
        waits = waits + source
        source_layer = source_layer + source * number_of(layer, r, len(routed))
        source_slot = source_slot + source * ranks[r]
        wanted = jnp.maximum(wanted, routed[r] * before(layer, 0, r))
    status = jnp.where(waits > 0.5, WAITS, READY)
    full = sum(jnp.where(rank > few, 1.0, 0.0) for rank in ranks)
    deep = jnp.where(sum(routed) > 2.5, 1.0, 0.0)
    counts = [jnp.zeros_like(deep) for _ in routed]
    for r, row in enumerate(routed):
        later = jnp.zeros_like(row)
        for other, other_row in enumerate(routed):
            if other != r:
                later = jnp.maximum(later, other_row * before(layer, r, other))
        for place in range(len(counts)):
            counts[place] = counts[place] + row * later * jnp.where((layer ^ r) == place, 1.0, 0.0)
    gates = gates_ref[...]
    high = gates.astype(bf16).astype(f32)
    named = {STATUS: status, SOURCE_LAYER: source_layer, SOURCE_SLOT: source_slot, WANTED: wanted}
    named.update({FULL: full, DEEP: deep})
    named.update({COUNTS + place: row for place, row in enumerate(counts)})
    for expert in range(gates.shape[0]):
        named[GATES + expert] = high[expert:expert + 1]
        named[GATES + gates.shape[0] + expert] = (gates - high)[expert:expert + 1]
    last = -(-(max(named) + 1) // 8) * 8
    empty = jnp.zeros_like(deep)
    table = [named.get(number, empty) for number in range(last)]
    table = stack_rows(table + [jnp.zeros((LANES - last, deep.shape[1]), f32)]).astype(bf16)
    select = selection(ranks[0] - skip, count)
    left = stack_rows([select, jnp.ones_like(select)]).astype(bf16)
    both = lax.dot_general(left, table, (((1,), (1,)), ((), ())), preferred_element_type=f32)
    lane = iota((count, LANES), 1)
    by_column = jnp.logical_or(lane == FULL, lane == DEEP)
    by_column = jnp.logical_or(by_column, jnp.logical_and(lane >= COUNTS, lane < GATES))
    extra = jnp.where(by_column, both[count:], both[:count])
    extra = jnp.where(lane == DEVICE, jnp.full((count, LANES), member + 1, jnp.int32).astype(f32), extra)
    extra = jnp.where(lane == SLOT, (iota((count, LANES), 0) + (1 + skip)).astype(f32), extra)
    payload_ref[:, :width] = raw_ref[...]
    payload_ref[:, width:] = extra.astype(bf16)


def distances(half):
    return [2 * q for q in range(half)] + [2 * q + 1 for q in range(half)]


def stack_body(half, *refs):
    near, pair_ref, rows_ref = refs[:half], refs[half], refs[half + 1]
    blocks = [ref[...] for ref in near] + [pair_ref[q] for q in range(half)]
    count = blocks[0].shape[0]
    if count % 16 == 0:
        for place, block in enumerate(blocks):
            rows_ref[place * count:(place + 1) * count] = block
    else:
        rows_ref[...] = stack_rows([block.astype(f32) for block in blocks]).astype(bf16)


def pair_body(*refs):
    out_ref = refs[-1]
    for q in range(out_ref.shape[0]):
        out_ref[q] = refs[q][...]


def more_stack_body(half, rows_ref, *refs):
    near, pair_ref, into_ref = refs[:half], refs[half], refs[half + 1]
    more = [ref[...] for ref in near] + [pair_ref[q] for q in range(half)]
    count = more[0].shape[0]
    if count % 16 == 0:
        for place, block in enumerate(more):
            into_ref[2 * place * count:(2 * place + 1) * count] = rows_ref[place * count:(place + 1) * count]
            into_ref[(2 * place + 1) * count:(2 * place + 2) * count] = block
        return
    rows = rows_ref[...].astype(f32)
    stacked = []
    for place, block in enumerate(more):
        stacked += [rows[place * count:(place + 1) * count], block.astype(f32)]
    into_ref[...] = stack_rows(stacked).astype(bf16)


def first_pass_body(half, sections, count, flight, *refs):
    gathered, refs = refs[:half + 1], refs[half + 1:]
    gain_ref, gate_ref, up_ref, down_ref, rows_ref, mode_ref, part_ref, chosen_ref, sent_ref = refs
    stack_body(half, *gathered, rows_ref)
    pass_body(count, flight, rows_ref, gain_ref, gate_ref, up_ref, down_ref, part_ref, chosen_ref, sent_ref)
    extra = rows_ref[:, gain_ref.shape[1]:].astype(f32)
    most = jnp.max(extra, axis=0, keepdims=True)
    total = jnp.sum(jnp.where(lane_of(extra, SLOT) == 1.0, extra, 0.0), axis=0, keepdims=True)
    total = jnp.max(total[:, COUNTS:COUNTS + sections], axis=1, keepdims=True)
    wanted_count = part_ref.shape[0]
    mode = jnp.where(total > wanted_count // 4, 1, 0) + jnp.where(total > wanted_count // 2, 1, 0)
    again = jnp.where(total > wanted_count // 2, 4, 3)
    again = jnp.where(total > wanted_count, again, jnp.where(lane_of(most, DEEP) > 0.5, again, mode))
    mode_ref[...] = jnp.where(lane_of(most, FULL) > 0.5, 5, again)


def activated(rows, gate_ref, up_ref):
    gate = jnp.dot(rows, gate_ref[...], preferred_element_type=f32)
    up = jnp.dot(rows, up_ref[...], preferred_element_type=f32)
    return gate / (1.0 + jnp.exp(-gate)) * up


def weight_of(extra, member, flight):
    lane = iota(extra.shape, 1)
    expert = member // GROUP
    mine = jnp.logical_or(lane == GATES + expert, lane == GATES + flight + expert)
    return jnp.sum(jnp.where(mine, extra, 0.0), axis=1, keepdims=True)


def pass_body(count, flight, rows_ref, gain_ref, gate_ref, up_ref, down_ref, part_ref, chosen_ref, sent_ref):
    member = whereabouts()[1]
    width = gain_ref.shape[1]
    wanted_count = part_ref.shape[0]
    extra = rows_ref[:, width:].astype(f32)
    wanted = lane_of(extra, WANTED)
    eligible = jnp.where(lane_of(extra, STATUS) == READY, wanted, 0.0)
    number = lane_of(extra, DEVICE) * count + lane_of(extra, SLOT)
    upto = number <= across(number)
    rank = jnp.sum(jnp.where(upto, eligible, 0.0), axis=0, keepdims=True) * across(eligible)
    select = selection(rank, wanted_count)
    chosen = jnp.dot(select.astype(bf16), rows_ref[...], preferred_element_type=f32)
    taken = jnp.sum(select, axis=0, keepdims=True)
    more = jnp.max(across(wanted) - taken, axis=1, keepdims=True)
    sent_ref[...] = taken
    lanes = chosen[:, width:]
    lane = iota(lanes.shape, 1)
    chosen_ref[:, :width] = chosen[:, :width].astype(bf16)
    chosen_ref[:, width:] = jnp.where(lane == MORE, more, lanes).astype(bf16)
    weight = weight_of(lanes, member, flight)
    hidden = activated(normalized(chosen[:, :width], gain_ref[...]), gate_ref, up_ref)
    if flight > 1:
        hidden = jnp.where(weight > 0.0, hidden, 0.0)
    share = jnp.dot(hidden.astype(bf16), down_ref[...], preferred_element_type=f32) * weight
    part_ref[...] = share.astype(bf16)


def added_body(a_ref, b_ref, out_ref):
    out_ref[...] = (a_ref[...].astype(f32) + b_ref[...].astype(f32)).astype(bf16)


def changed_body(*refs):
    shares, chosen_ref, out_ref = refs[:-2], refs[-2], refs[-1]
    width = shares[0].shape[1]
    sums = [ref[...].astype(f32) for ref in shares]
    while len(sums) > 1:
        sums = [sums[i] + sums[i + 1] for i in range(0, len(sums), 2)]
    out_ref[:, :width] = (chosen_ref[:, :width].astype(f32) + sums[0]).astype(bf16)
    out_ref[:, width:] = chosen_ref[:, width:]


def by_chunks(size, run):
    if size <= CHUNK:
        run(slice(0, size))
        return

    @pl.loop(0, size // CHUNK)
    def _(i):
        run(pl.ds(pl.multiple_of(i * CHUNK, CHUNK), CHUNK))


def apply_body(sections, rows_ref, sent_ref, *refs):
    changed, into_ref, more_ref = refs[:sections], refs[sections], refs[sections + 1]
    layer = whereabouts()[0]
    width = rows_ref.shape[1] - LANES
    names = [ref[:, width:].astype(f32) for ref in changed]
    fresh = stack_rows([ref[:, :width].astype(f32) for ref in changed[1:]]).astype(bf16)
    columns = [(across(lane_of(name, DEVICE)), across(lane_of(name, SLOT))) for name in names]
    if more_ref is not None:
        more = names[0]
        for name in names[1:]:
            more = jnp.maximum(more, name)
        more_ref[...] = jnp.max(lane_of(more, MORE), axis=0, keepdims=True)
    size = rows_ref.shape[0]
    taken = sent_ref[...]

    def run(part):
        extra = rows_ref[part, width:].astype(f32)
        waits = jnp.where(lane_of(extra, STATUS) == WAITS, 1.0, 0.0)
        matches = []
        for r in range(1, sections):
            device, slot = columns[r]
            match = jnp.where(lane_of(extra, DEVICE) == device, waits, 0.0)
            match = match * jnp.where(lane_of(extra, SOURCE_SLOT) == slot, 1.0, 0.0)
            from_it = jnp.where(lane_of(extra, SOURCE_LAYER) == number_of(layer, r, sections), 1.0, 0.0)
            matches.append(match * from_it)
        match = jnp.concatenate(matches, axis=1)
        arrived = jnp.max(match, axis=1, keepdims=True)
        new = jnp.dot(match.astype(bf16), fresh, preferred_element_type=f32)
        old = rows_ref[part, :width].astype(f32)
        into_ref[part, :width] = jnp.where(arrived > 0.5, new, old).astype(bf16)
        lane = iota(extra.shape, 1)
        extra = jnp.where(jnp.logical_and(lane == STATUS, arrived > 0.5), READY, extra)
        if size <= CHUNK:
            own = iota((size, size), 0) == iota((size, size), 1)
            gone = jnp.sum(jnp.where(own, taken, 0.0), axis=1, keepdims=True)
        else:
            first = part.start
            row = iota((CHUNK, size), 0) + first == iota((CHUNK, size), 1)
            gone = jnp.sum(jnp.where(row, taken, 0.0), axis=1, keepdims=True)
        extra = jnp.where(jnp.logical_and(lane == WANTED, gone > 0.5), 0.0, extra)
        into_ref[part, width:] = extra.astype(bf16)

    by_chunks(size, run)


def changed_final_body(half, sections, flight, rows_ref, sent_ref, *refs):
    changed, rest, into_ref = refs[:sections], refs[sections:-1], refs[-1]
    apply_body(sections, rows_ref, sent_ref, *changed, into_ref, None)
    final_body(half, flight, into_ref, *rest)


def final_body(
    half, flight, rows_ref, gain_ref, gate_ref, up_ref, down_ref,
    hidden_ref, raw_ref, near_ref, soon_ref, late_ref, ordered_ref
):
    member = whereabouts()[1]
    width = gain_ref.shape[1]
    units = hidden_ref.shape[1]
    size = rows_ref.shape[0]
    side = size // 2
    count = raw_ref.shape[0]
    raw_ref[...] = rows_ref[:, :width].astype(f32)[:count].astype(bf16) if size <= CHUNK else rows_ref[:count, :width]
    hidden_rows = []

    def run(part, of_part=None):
        extra = rows_ref[part, width:].astype(f32)
        weight = weight_of(extra, member, flight)
        hidden = activated(normalized(rows_ref[part, :width].astype(f32), gain_ref[...]), gate_ref, up_ref)
        if flight > 1:
            hidden = jnp.where(weight > 0.0, hidden, 0.0)
        share = jnp.dot(hidden.astype(bf16), down_ref[...], preferred_element_type=f32) * weight
        return hidden, share

    if size <= CHUNK:
        hidden, share = run(slice(0, size))
        near_ref[...] = share[:side].astype(bf16)
        late_ref[...] = share[side:side + side // 2].astype(bf16)
        soon_ref[:, :width] = share[side + side // 2:].astype(bf16)
        for place, r in enumerate(distances(half)):
            ordered_ref[member ^ r, :count] = hidden[place * count:(place + 1) * count]
    else:
        blocks = CHUNK // count

        def part_run(first, size, into_ref, block, odd):
            @pl.loop(0, size // CHUNK)
            def _(i):
                at = pl.multiple_of(i * CHUNK, CHUNK)
                hidden, share = run(pl.ds(pl.multiple_of(first + at, CHUNK), CHUNK))
                into_ref[pl.ds(at, CHUNK), :width] = share.astype(bf16)
                for b in range(blocks):
                    distance = 2 * (block + i * blocks + b) + odd
                    ordered_ref[member ^ distance] = hidden[b * count:(b + 1) * count]

        part_run(0, side, near_ref, 0, 0)
        part_run(side, side // 2, late_ref, 0, 1)
        part_run(side + side // 2, side // 2, soon_ref, half // 2, 1)
    ordered_rows = stack_rows([ordered_ref[source, :count] for source in range(2 * half)])
    hidden_rows = ordered_rows.astype(bf16)
    hidden_ref[...] = hidden_rows
    quarter = side // 2
    for i in range(4):
        rows_of = slice(i * quarter, (i + 1) * quarter)
        values = ordered_rows[rows_of].astype(bf16) if quarter % 16 else hidden_rows[rows_of]
        soon_ref[:, width + i * units:width + (i + 1) * units] = values


def regrouped(rows, count):
    return jnp.concatenate([rows[i:i + count] for i in range(0, rows.shape[0], count)], axis=1)


def spread(block, units):
    return stack_rows([block[:, i:i + units] for i in range(0, block.shape[1], units)])


def their_hidden(soon_ref, width, units):
    behind = soon_ref[:, width:].astype(f32)
    return stack_rows([behind[:, i:i + units] for i in range(0, behind.shape[1], units)])


def paired_body(half, first, number, near_ref, far_ref, soon_ref, hidden_ref, *out_refs):
    width = near_ref.shape[1]
    units = hidden_ref.shape[1]
    count = near_ref.shape[0] // half
    mine = near_ref[...].astype(f32)[first * count:(first + number) * count]
    total = mine + far_ref[:, :width].astype(f32)
    both = None
    for q, ref in enumerate(out_refs):
        ref[:, :width] = total[q * count:(q + 1) * count].astype(bf16)
        if ref.shape[1] > width:
            if both is None:
                both = [hidden_ref[...].astype(f32), their_hidden(soon_ref, width, units)]
                both = jnp.concatenate([regrouped(rows, count) for rows in both], axis=1).astype(bf16)
            ref[:, width:] = both


def combine_body(half, *refs):
    shares, raw_ref, out_ref = refs[:half], refs[half], refs[-1]
    width = raw_ref.shape[1]
    update = shares[0][:, :width].astype(f32)
    for ref in shares[1:]:
        update = update + ref[:, :width].astype(f32)
    out_ref[...] = (raw_ref[...].astype(f32) + update).astype(bf16)


def plan_body(sections, count, *refs):
    tables = refs[:sections]
    state_ref, _, select_ref, base_ref = refs[sections:]
    layer = whereabouts()[0]
    routed = [ref[...].astype(f32) for ref in tables]
    shown = [row * jnp.where((layer ^ r) <= layer, 1.0, 0.0) for r, row in enumerate(routed)]
    select = []
    for r, rank in enumerate(ranked(routed)):
        later = jnp.zeros_like(rank)
        for other, row in enumerate(shown):
            if other != r:
                later = jnp.maximum(later, row * before(layer, r, other))
        select.append(selection(jnp.where(shown[r] > 0.5, rank * (1.0 - later), 0.0), count))
    select = stack_rows(select).astype(bf16)
    size = select.shape[0]
    same = (iota((size, size), 0) == iota((size, size), 1)).astype(f32).astype(bf16)
    over = (((0,), (0,)), ((), ()))
    turned = lax.dot_general(select, same, over, preferred_element_type=f32)
    select_ref[...] = turned.astype(bf16)
    hit = jnp.sum(turned, axis=1, keepdims=True)
    base_ref[...] = jnp.where(hit > 0.5, 0.0, state_ref[...].astype(f32)).astype(bf16)


def merge_body(sections, *refs):
    blocks = refs[:sections]
    select_ref, base_ref, into_ref, held_ref, sems = refs[sections:]
    width = base_ref.shape[1]
    rows = stack_rows([block[...].astype(f32) for block in blocks]).astype(bf16)
    copies = []
    chunks = sems.shape[0]
    step = width // chunks
    for i in range(chunks):
        part = slice(i * step, (i + 1) * step)
        fresh = jnp.dot(select_ref[...], rows[:, part], preferred_element_type=f32)
        held_ref[:, part] = (fresh + base_ref[:, part].astype(f32)).astype(bf16)
        copies.append(pltpu.make_async_copy(held_ref.at[:, part], into_ref.at[:, part], sems.at[i]))
        copies[-1].start()
    for copy in copies:
        copy.wait()


def gram_body(scale, width, mine_ref, far_ref, *refs):
    others, (out_ref, held_ref, sem) = refs[:-3], refs[-3:]
    member = whereabouts()[1] % GROUP
    mine = mine_ref[...]
    size, units = mine.shape
    blocks = [mine, their_hidden(far_ref, width, units).astype(bf16)]
    for ref in others:
        both = spread(ref[:, width:].astype(f32), units).astype(bf16)
        blocks += [both[:size], both[size:]]
    for r, block in enumerate(blocks):
        term = scale * lax.dot_general(
            mine, block, (((0,), (0,)), ((), ())), preferred_element_type=f32
        )
        held_ref[:, pl.ds(pl.multiple_of((member ^ r) * units, units), units)] = term
    copy = pltpu.make_async_copy(held_ref, out_ref, sem)
    copy.start()
    copy.wait()


def passed(value, axis, r):
    return lax.ppermute(value, axis, [(i, i ^ r) for i in range(lax.axis_size(axis))])


def exchanged(value, axis):
    return [value] + [passed(value, axis, r) for r in range(1, lax.axis_size(axis))]


def shards(stream_in, gain, w_gate, w_up, w_down, routes, gates):
    fronts, tok_rows, width = stream_in.shape
    units = w_gate.shape[2]
    sections = lax.axis_size("layer")
    devices = lax.axis_size("expert")
    flight = devices // GROUP
    half = devices // 2
    tokens = fronts * tok_rows
    few = FEW * flight
    shape = jax.ShapeDtypeStruct
    state = stream_in.reshape(tokens, width)
    routes = jnp.swapaxes(routes[0], 1, 2)
    gates = jnp.swapaxes(gates[0], 1, 2)
    w_gate, w_up, w_down = w_gate[0], w_up[0], w_down[0]
    scale = 1.0 / (fronts * CAP)
    mib = 2**20
    chunks = next(c for c in (7, 8, 4, 2, 1) if width % (c * LANES) == 0)

    def raw_of(count, skip):
        return call(
            functools.partial(rows_body, skip),
            shape((count, width), bf16),
            2,
            traffic=2 * tokens * width,
            limit=8 * mib,
        )(table, state)

    def payload_of(raw, gate_weights, skip):
        count = raw.shape[0]
        return call(
            functools.partial(meta_body, few, skip),
            shape((count, width + LANES), bf16),
            sections + 2,
            limit=8 * mib,
        )(*tables, gate_weights, raw)

    def near_of(payload):
        return [payload] + [passed(payload, "expert", r) for r in range(2, devices, 2)]

    def pair_of(near, after=()):
        stacked = call(
            pair_body,
            shape((half, *near[0].shape), bf16),
            half + len(after),
            traffic=4 * half * near[0].size,
            limit=4 * mib + 16 * half * near[0].size,
        )(*near, *after)
        return passed(stacked, "expert", 1)

    def held(after, *weights):
        return call(
            held_body,
            tuple(shape(w.shape, bf16) for w in weights),
            1,
            streamed=len(weights),
            scratch=[pltpu.SemaphoreType.DMA((len(weights),))],
            traffic=4 * sum(w.size for w in weights),
            limit=2 * sum(w.size for w in weights) + 2 * mib,
        )(after, *weights)

    def pass_shapes(size, wanted):
        return (
            shape((wanted, width), bf16),
            shape((wanted, width + LANES), bf16),
            shape((1, size), f32),
        )

    def pass_limit(size):
        return 8 * mib + 12 * size * width + 32 * size * size

    def summed(part, chosen):
        steps = [[1 << b] for b in range(devices.bit_length() - 1)]
        if devices == GROUP:
            steps = [[1], list(range(2, devices, 2))]
        for (distance,) in steps[:-1]:
            part = call(added_body, shape(part.shape, bf16), 2, traffic=6 * part.size)(
                part, passed(part, "expert", distance)
            )
        others = [passed(part, "expert", distance) for distance in steps[-1]]
        changed = call(
            changed_body,
            shape(chosen.shape, bf16),
            2 + len(others),
            traffic=8 * chosen.size,
            limit=2 * mib + 32 * chosen.size,
        )(part, *others, chosen)
        return exchanged(changed, "layer")

    def apply_limit(size, wanted):
        return 8 * mib + 16 * sections * wanted * width + 8 * size * width

    def applied(rows, sent, changed):
        size, wanted = rows.shape[0], changed[0].shape[0]
        return call(
            functools.partial(apply_body, sections),
            (shape(rows.shape, bf16), shape((1, 1), f32)),
            2 + sections,
            flops=2 * size * sections * wanted * width,
            traffic=4 * size * width,
            limit=apply_limit(size, wanted),
        )(rows, sent, *changed)

    def passes(rows, wanted, weights):
        size = rows.shape[0]
        count = size // devices
        part, chosen, sent = call(
            functools.partial(pass_body, count, flight),
            pass_shapes(size, wanted),
            5,
            flops=6 * wanted * width * units,
            traffic=2 * size * width,
            limit=pass_limit(size),
        )(rows, gain, *weights)
        return applied(rows, sent, summed(part, chosen))

    def finish(rows, count, weights, sent=None, changed=()):
        size = devices * count
        side = size // 2
        body = functools.partial(final_body, half, flight)
        operands = (rows,)
        more_scratch = []
        if changed:
            body = functools.partial(changed_final_body, half, sections, flight)
            operands = (rows, sent, *changed)
            more_scratch = [pltpu.VMEM(rows.shape, bf16)]
        hidden, raw, near, soon, late = call(
            body,
            (
                shape((size, units), bf16),
                shape((count, width), bf16),
                shape((side, width), bf16),
                shape((side // 2, width + 4 * units), bf16),
                shape((side // 2, width), bf16),
            ),
            5 + (1 + sections if changed else 0),
            scratch=[pltpu.VMEM((devices, -(-count // 8) * 8, units), f32)] + more_scratch,
            flops=6 * size * width * units,
            traffic=6 * width * units,
            limit=8 * mib
            + 24 * min(size, CHUNK) * width
            + 4 * size * width
            + 16 * size * units
            + (apply_limit(size, changed[0].shape[0]) if changed else 0),
        )(*operands, gain, *weights)
        soon = passed(soon, "expert", 1)
        late = passed(late, "expert", 1)
        behind = 2 * devices * units

        def paired(first, far):
            return call(
                functools.partial(paired_body, half, first, half // 2),
                tuple(
                    shape((count, width + (behind if 0 < q < GROUP // 2 else 0)), bf16)
                    for q in range(first, first + half // 2)
                ),
                4,
                traffic=3 * side * width,
                limit=4 * mib + 20 * side * width + 24 * count * behind,
            )(near, far, soon, hidden)

        farther = paired(half // 2, soon)
        arrived = [passed(sums, "expert", 2 * (half // 2 + q)) for q, sums in enumerate(farther)]
        closer = paired(0, late)
        arrived = [passed(closer[q], "expert", 2 * q) for q in range(1, half // 2)] + arrived
        arrived = [closer[0]] + arrived
        select, base = call(
            functools.partial(plan_body, sections, count),
            (shape((tokens, sections * count), bf16), shape((tokens, width), bf16)),
            sections + 2,
            traffic=4 * tokens * width,
            limit=8 * mib,
        )(*tables, state, farther[0])
        fresh = call(
            functools.partial(combine_body, half),
            shape((count, width), bf16),
            half + 2,
            traffic=2 * side * width,
            limit=2 * mib + 16 * count * width + 6 * count * behind,
        )(*arrived, raw, select)
        blocks = exchanged(fresh, "layer")
        gram = call(
            functools.partial(gram_body, scale, width),
            shape((units, GROUP * units), f32),
            2 + GROUP // 2 - 1,
            scratch=[pltpu.VMEM((units, GROUP * units), f32), pltpu.SemaphoreType.DMA(())],
            placed=HBM,
            flops=2 * size * units * units * GROUP,
            traffic=4 * units * units * GROUP,
            limit=8 * mib + 64 * size * units,
        )(hidden, soon, *arrived[1:GROUP // 2])
        new_state = call(
            functools.partial(merge_body, sections),
            shape((tokens, width), bf16),
            sections + 2,
            scratch=[pltpu.VMEM((tokens, width), bf16), pltpu.SemaphoreType.DMA((chunks,))],
            placed=HBM,
            traffic=4 * tokens * width,
            limit=8 * mib + 16 * sections * count * width,
        )(*blocks, select, base)
        return new_state, gram

    def looped(rows, more, wanted, weights):
        _, rows = lax.while_loop(
            lambda carry: carry[0][0, 0] > 0.5,
            lambda carry: passes(carry[1], wanted, weights)[::-1],
            (more, rows),
        )
        return finish(rows, rows.shape[0] // devices, weights)

    table, kept_routes = call(
        functools.partial(table_body, flight), (shape((1, tokens), bf16), shape(routes.shape, routes.dtype)), 1
    )(routes)
    tables = exchanged(table, "layer")
    raw = raw_of(few, 0)
    gate_weights = call(gates_body, shape((flight, tokens), f32), 2)(kept_routes, gates)
    payload = payload_of(raw, gate_weights, 0)
    near = near_of(payload)
    early = held(payload, w_gate)
    pair = pair_of(near, early)
    weights = *early, *held(near[1], w_up, w_down)
    size = devices * few
    rows, mode, part, chosen, sent = call(
        functools.partial(first_pass_body, half, sections, few, flight),
        (shape((size, width + LANES), bf16), shape((1, 1), jnp.int32)) + pass_shapes(size, 2 * few),
        half + 5,
        flops=12 * few * width * units,
        traffic=4 * size * width,
        limit=pass_limit(size),
    )(*near, pair, gain, *weights)

    def once(share):
        def run(rows, part, chosen, sent, gate_weights, *weights):
            wanted = part.shape[0] // share
            return finish(rows, few, weights, sent, summed(part[:wanted], chosen[:wanted]))

        return run

    def again(share):
        def run(rows, part, chosen, sent, gate_weights, *weights):
            wanted = part.shape[0] // share
            rows, more = applied(rows, sent, summed(part[:wanted], chosen[:wanted]))
            return looped(rows, more, few // 2, weights)

        return run

    def filled(rows, part, chosen, sent, gate_weights, *weights):
        most = fronts * CAP * flight
        near = near_of(payload_of(raw_of(most - few, few), gate_weights, few))
        rows = call(
            functools.partial(more_stack_body, half),
            shape((devices * most, width + LANES), bf16),
            half + 2,
            traffic=4 * devices * most * width,
            limit=4 * mib + 16 * devices * most * width,
        )(rows, *near, pair_of(near))
        rows, more = passes(rows, 2 * few, weights)
        return looped(rows, more, 2 * few, weights)

    shares = (4, 2, 1) if size <= CHUNK else (1, 1, 1)
    branches = [once(share) for share in sorted(set(shares), reverse=True)]
    branches += [again(share) for share in sorted(set(shares[1:]), reverse=True)]
    branches.append(filled)
    mode = mode[0, 0] if size <= CHUNK else jnp.maximum(mode[0, 0] - 1, 0) // 2
    state, gram = lax.switch(
        mode, branches, rows, part, chosen, sent, gate_weights, *weights
    )
    return state.reshape(1, fronts, tok_rows, width), gram[None]


def solution(mesh):
    return jax.shard_map(
        shards,
        mesh=mesh,
        in_specs=(
            P(None, "expert", None),
            P("layer", None),
            P("layer", None, "expert"),
            P("layer", None, "expert"),
            P("layer", "expert", None),
            P("layer", None, "expert", None),
            P("layer", None, "expert", None),
        ),
        out_specs=(P("layer", None, "expert", None), P("layer", "expert", None)),
        check_vma=False,
    )
```
